256 devices in a mesh: view: 8 (over z), tile: 32 (over x, y, core).
Axes of the slice: x: 4, y: 4, z: 8, core: 2. Of those that a mesh axis runs over, the one named last changes fastest.
Arguments:
- features: float32 [2048, 64, 128], P(('view', 'tile')), may hold values from -24 to 24
- moment_first: float32 [2048, 64, 128], P(('view', 'tile')), may hold values from -0.6 to 0.6
- moment_second: float32 [2048, 64, 128], P(('view', 'tile')), may hold values from 0.0001 to 0.1
- positions: float32 [2048, 3, 128], P(('view', 'tile')), may hold values from 0 to 1
- scales: float32 [2048, 128], P(('view', 'tile')), may hold values from 1.5 to 5
- opacity: float32 [2048, 128], P(('view', 'tile')), may hold values from -7 to -3
- cameras_first: float32 [8, 2, 4], P('view'), may hold values from -4 to 16
- shift_first: float32 [8, 512, 2], P('view', 'tile'), may hold values from -2 to 2
- lists_first: int32 [8, 512, 8], P('view', 'tile'), may hold values from 0 to 255, as said below
- loads_first: int32 [8, 512], P('view', 'tile'), may hold values from 1 to 8
- target: bfloat16 [8, 512, 64, 256], P('view', 'tile'), may hold values from -12 to 12
- owner_after: int32 [2048], P(('view', 'tile')), may hold values from 0 to 7, as said below
- cameras_second: float32 [8, 2, 4], P('view'), may hold values from -4 to 16
- shift_second: float32 [8, 512, 2], P('view', 'tile'), may hold values from -2 to 2
- lists_second: int32 [8, 512, 8], P('view', 'tile'), may hold values from 0 to 255, as said below
- loads_second: int32 [8, 512], P('view', 'tile'), may hold values from 1 to 8
Outputs:
- image_second: float32 [8, 512, 64, 256], P('view', 'tile')
- new_features: float32 [2048, 64, 128], P(('view', 'tile'))
- new_first: float32 [2048, 64, 128], P(('view', 'tile'))
- new_second: float32 [2048, 64, 128], P(('view', 'tile'))
The draws below stay inside these ranges and needn't reach their ends.
Inputs may be any that keep to these rules, and one draw needn't show every extreme that they name: `lists_first`: on each device, at most 6 of its list entries name bins of any one device of its view group, and some device of the group is named exactly 6 times. `lists_second`: on each device, at most 6 of its list entries name bins of any one device of its view group after the move, and some device of the group is named exactly 6 times. `owner_after`: each device's 8 entries name every view group exactly 1 times.
All inputs are finite; a program needn't handle non-finite values.
Results may differ from the reference program's by a relative error of at most 0.0015.
The reference program's roundings to bfloat16 on the way count: a program that leaves them out, or rounds other values in their place, can miss the bound.
Values may be sent and summed in bfloat16 or wider, within the bound.
No kernel may reach another device: no remote copies, remote signals or barrier semaphores. Data moves between devices by JAX's collectives and lax.ppermute only.
A program may use at most 64 MiB of HBM per device.

```python
import math
import jax
import jax.numpy as jnp
from jax import lax

C = 64
GB = 128
TILE_SIDE = 16
PIX = 256
LBLK = 8
TILES_DEV = 16
BINS_DEV = 8
MOST = 6
BPV = 1
ROW_BINS = 256
BINS = 2048
TILES = 512
N_VIEW = 8
N_TILE = 32


def route_lists(key):
    renderers = N_VIEW * N_TILE
    entries = TILES_DEV * LBLK
    slot_total = N_TILE * MOST
    keys = jax.random.split(key, 4)
    scores = jax.vmap(lambda subkey: jax.random.permutation(subkey, slot_total))(jax.random.split(keys[0], renderers))
    chosen_owner = jax.random.randint(keys[1], (renderers, 1), 0, N_TILE)
    owner_of_slot = jnp.arange(slot_total, dtype=jnp.int32) // MOST
    boosted = scores.astype(jnp.int32) + slot_total * (owner_of_slot[None, :] == chosen_owner).astype(jnp.int32)
    picked = jnp.argsort(-boosted, axis=1, stable=True)[:, :entries]
    shuffle = jax.vmap(lambda subkey: jax.random.permutation(subkey, entries))(jax.random.split(keys[2], renderers))
    picked = jnp.take_along_axis(picked, shuffle, axis=1)
    owners = picked // MOST
    within = jax.random.randint(keys[3], (renderers, entries), 0, BINS_DEV)
    return (owners * BINS_DEV + within).reshape(N_VIEW, N_TILE * TILES_DEV, LBLK).astype(jnp.int32)


def camera_draw(key):
    noise = jax.random.uniform(key, (N_VIEW, 2, 4), jnp.float32, -1.0, 1.0)
    base = jnp.array([[14.0, 0.0, 0.0, 1.0], [0.0, 14.0, 0.0, 1.0]], jnp.float32)
    spread = jnp.array([[1.0, 1.0, 4.0, 1.0], [1.0, 1.0, 4.0, 1.0]], jnp.float32)
    return base[None] + spread[None] * noise


def draw_lists_first(key, part):
    key = jax.random.fold_in(key, 11)
    return route_lists(key)


def draw_lists_second(key, part):
    key = jax.random.fold_in(key, 12)
    return route_lists(key)


def draw_owner_after(key, part):
    key = jax.random.fold_in(key, 13)
    device_total = N_VIEW * N_TILE
    base = jnp.arange(BINS_DEV, dtype=jnp.int32) // BPV
    rows = jax.vmap(lambda subkey: jax.random.permutation(subkey, base))(jax.random.split(key, device_total))
    return rows.reshape(-1).astype(jnp.int32)


def draw_cameras_first(key, part):
    key = jax.random.fold_in(key, 14)
    return camera_draw(key)


def draw_cameras_second(key, part):
    key = jax.random.fold_in(key, 15)
    return camera_draw(key)


def plant(values, key, low, largest):
    extent = values.shape
    place = [jax.random.randint(jax.random.fold_in(key, axis), (), 0, extent[axis]) for axis in range(len(extent))]
    values = values.at[tuple(place)].set(low)
    longest = extent.index(max(extent))
    place[longest] = (place[longest] + 1) % extent[longest]
    return values.at[tuple(place)].set(largest)


def levels(stream_key, dims, shards, least, high):
    def one(dim, blocks):
        heights = jax.random.uniform(jax.random.fold_in(jax.random.fold_in(stream_key, 6), dim), (blocks,), jnp.float32, least / len(shards), high / len(shards))
        return jnp.repeat(jnp.exp(heights), dims[dim] // blocks).reshape((-1,) + (1,) * (len(dims) - dim - 1))

    level = one(*shards[0])
    for cut in shards[1:]:
        level = level * one(*cut)
    return level


def gaussian(rng, shape, scale, reach, shards=(), kind=jnp.bfloat16):
    result = scale * jax.random.normal(rng, shape, jnp.float32)
    if shards:
        result = result * levels(rng, shape, shards, -0.22, 0.18)
    return jnp.clip(result, -reach, reach).astype(kind)


def setup_inputs(seed: int = 0) -> dict:
    streams_of = jax.random.split(jax.random.key(seed), 17)
    features = gaussian(streams_of[0], (BINS, C, GB), 4.0, 24.0, ((0, 256),), jnp.float32)
    moment_first = gaussian(streams_of[1], (BINS, C, GB), 0.1, 0.6, ((0, 256),), jnp.float32)
    moment_second = jnp.clip(jnp.exp(math.log(0.1) - 6.9077553 * jax.random.uniform(streams_of[2], (BINS, C, GB), jnp.float32) ** levels(streams_of[2], (BINS, C, GB), ((0, 256),), -0.2, 0.2)), 0.0001, 0.1)
    positions = jnp.clip(1.0 * jax.random.uniform(streams_of[3], (BINS, 3, GB), jnp.float32) ** levels(streams_of[3], (BINS, 3, GB), ((0, 256),), -0.2, 0.2), 0.0, 1.0)
    scales = jnp.clip(jnp.exp(math.log(5.0) - 1.2039728 * jax.random.uniform(streams_of[4], (BINS, GB), jnp.float32) ** levels(streams_of[4], (BINS, GB), ((0, 256),), -0.2, 0.2)), 1.5, 5.0)
    opacity = jnp.clip(-7.0 + 4.0 * jax.random.uniform(streams_of[5], (BINS, GB), jnp.float32) ** levels(streams_of[5], (BINS, GB), ((0, 256),), -0.2, 0.2), -7.0, -3.0)
    cameras_first = draw_cameras_first(jax.random.fold_in(streams_of[16], 71), 0)
    shift_first = jnp.clip(jax.random.uniform(streams_of[7], (N_VIEW, TILES, 2), jnp.float32, -2.0, 2.0) * levels(streams_of[7], (N_VIEW, TILES, 2), ((0, 8), (1, 32)), -0.4, 0.0), -2.0, 2.0)
    lists_first = draw_lists_first(jax.random.fold_in(streams_of[16], 71), 0)
    loads_first = plant(jax.random.randint(streams_of[9], (N_VIEW, TILES), 1, LBLK + 1), jax.random.fold_in(streams_of[9], 1), 1, LBLK).astype(jnp.int32)
    target = gaussian(streams_of[10], (N_VIEW, TILES, C, PIX), 2.0, 12.0, ((0, 8), (1, 32)))
    owner_after = draw_owner_after(jax.random.fold_in(streams_of[16], 71), 0)
    cameras_second = draw_cameras_second(jax.random.fold_in(streams_of[16], 71), 0)
    shift_second = jnp.clip(jax.random.uniform(streams_of[13], (N_VIEW, TILES, 2), jnp.float32, -2.0, 2.0) * levels(streams_of[13], (N_VIEW, TILES, 2), ((0, 8), (1, 32)), -0.4, 0.0), -2.0, 2.0)
    lists_second = draw_lists_second(jax.random.fold_in(streams_of[16], 71), 0)
    loads_second = plant(jax.random.randint(streams_of[15], (N_VIEW, TILES), 1, LBLK + 1), jax.random.fold_in(streams_of[15], 1), 1, LBLK).astype(jnp.int32)
    return {"features": features, "moment_first": moment_first, "moment_second": moment_second, "positions": positions, "scales": scales, "opacity": opacity, "cameras_first": cameras_first, "shift_first": shift_first, "lists_first": lists_first, "loads_first": loads_first, "target": target, "owner_after": owner_after, "cameras_second": cameras_second, "shift_second": shift_second, "lists_second": lists_second, "loads_second": loads_second}


beta_first = 0.9
beta_second = 0.999
learn_rate = 0.05
adam_epsilon = 1e-08
bias_first = 1.0 - 0.9 ** 10
bias_second = 1.0 - 0.999 ** 10

def project(positions, scales, opacity, camera):
    mean_x = camera[0, 0] * positions[:, 0] + camera[0, 1] * positions[:, 1] + camera[0, 2] * positions[:, 2] + camera[0, 3]
    mean_y = camera[1, 0] * positions[:, 0] + camera[1, 1] * positions[:, 1] + camera[1, 2] * positions[:, 2] + camera[1, 3]
    falloff = 0.5 / (scales * scales)
    opaque = jax.nn.sigmoid(opacity)
    return jnp.stack([mean_x, mean_y, falloff, opaque], axis=1).astype(jnp.bfloat16)

def block_weights(params, live_mask, offset, carried):
    pixel_ids = jnp.arange(TILE_SIDE * TILE_SIDE, dtype=jnp.int32)
    pixel_x = (pixel_ids % TILE_SIDE).astype(jnp.float32) + 0.5
    pixel_y = (pixel_ids // TILE_SIDE).astype(jnp.float32) + 0.5
    place_x = pixel_x[None, :] + offset[:, 0:1]
    place_y = pixel_y[None, :] + offset[:, 1:2]
    values = params.astype(jnp.float32)
    delta_x = place_x[:, :, None] - values[:, None, 0, :]
    delta_y = place_y[:, :, None] - values[:, None, 1, :]
    alphas = values[:, None, 3, :] * jnp.exp(-values[:, None, 2, :] * (delta_x * delta_x + delta_y * delta_y))
    alphas = jnp.where(live_mask[:, None, None], alphas, jnp.zeros_like(alphas))
    log_keep = jnp.log1p(-alphas)
    running = jnp.cumsum(log_keep, axis=2)
    transmit = jnp.exp(carried[:, :, None] + (running - log_keep))
    weights = (transmit * alphas).astype(jnp.bfloat16)
    return (weights, carried + running[:, :, -1])

def render_tiles(ent_params, ent_colors, live_counts, offset):
    tile_rows = ent_params.shape[1]

    def advance(state, inputs):
        carried, picture = state
        params, colors, block_index = inputs
        weights, carried = block_weights(params, block_index < live_counts, offset, carried)
        picture = picture + jnp.einsum('tcg,tpg->tcp', colors.astype(jnp.float32), weights.astype(jnp.float32))
        return ((carried, picture), None)
    initial = (jnp.zeros((tile_rows, PIX), jnp.float32), jnp.zeros((tile_rows, C, PIX), jnp.float32))
    blocks = jnp.arange(ent_params.shape[0], dtype=jnp.int32)
    (carried, picture), unused = lax.scan(advance, initial, (ent_params, ent_colors, blocks))
    return picture

def feature_grads(ent_params, live_counts, offset, residual):
    tile_rows = ent_params.shape[1]
    residual_wide = residual.astype(jnp.float32)

    def advance(carried, inputs):
        params, block_index = inputs
        weights, carried = block_weights(params, block_index < live_counts, offset, carried)
        pieces = jnp.einsum('tcp,tpg->tcg', residual_wide, weights.astype(jnp.float32))
        return (carried, pieces)
    blocks = jnp.arange(ent_params.shape[0], dtype=jnp.int32)
    carried, pieces = lax.scan(advance, jnp.zeros((tile_rows, PIX), jnp.float32), (ent_params, blocks))
    return pieces

def view_screen(positions, scales, opacity, cameras):
    return jax.vmap(project)(positions.reshape(N_VIEW, ROW_BINS, 3, GB), scales.reshape(N_VIEW, ROW_BINS, GB), opacity.reshape(N_VIEW, ROW_BINS, GB), cameras)

def grads_of_view(view_items):
    screen_row, colors_row, list_ids, live_counts, offset, target_view = view_items
    order_ids = list_ids.T
    ent_params = screen_row[order_ids]
    ent_colors = colors_row[order_ids]
    picture = render_tiles(ent_params, ent_colors, live_counts, offset)
    residual = (picture - target_view.astype(jnp.float32)).astype(jnp.bfloat16)
    pieces = feature_grads(ent_params, live_counts, offset, residual)
    flat_ids = order_ids.reshape(-1)
    return jnp.zeros((ROW_BINS, C, GB), jnp.float32).at[flat_ids].add(pieces.reshape(-1, C, GB))

def picture_of_view(view_items):
    screen_row, colors_row, list_ids, live_counts, offset = view_items
    order_ids = list_ids.T
    return render_tiles(screen_row[order_ids], colors_row[order_ids], live_counts, offset)

def relocate(array, target_pos):
    return jnp.zeros_like(array).at[target_pos].set(array)

def reference(features, moment_first, moment_second, positions, scales, opacity, cameras_first, shift_first, lists_first, loads_first, target, owner_after, cameras_second, shift_second, lists_second, loads_second):
    screen = view_screen(positions, scales, opacity, cameras_first)
    colors = features.astype(jnp.bfloat16).reshape(N_VIEW, ROW_BINS, C, GB)
    gradient = lax.map(grads_of_view, (screen, colors, lists_first, loads_first, shift_first, target))
    gradient = gradient.reshape(BINS, C, GB)
    first_new = beta_first * moment_first + (1.0 - beta_first) * gradient
    second_new = beta_second * moment_second + (1.0 - beta_second) * gradient * gradient
    stepped = features - learn_rate * (first_new / bias_first) / (jnp.sqrt(second_new / bias_second) + adam_epsilon)
    device_total = N_VIEW * N_TILE
    destination = owner_after.reshape(device_total, BINS_DEV).astype(jnp.int32)
    onehot = (destination[:, :, None] == jnp.arange(N_VIEW, dtype=jnp.int32)[None, None, :]).astype(jnp.int32)
    rank_in = lax.optimization_barrier(jnp.sum((jnp.cumsum(onehot, axis=1) - onehot) * onehot, axis=2))
    device_ids = jnp.arange(device_total, dtype=jnp.int32)[:, None]
    source_view = device_ids // N_TILE
    tile_ids = device_ids % N_TILE
    target_pos = ((destination * N_TILE + tile_ids) * BINS_DEV + source_view * BPV + rank_in).reshape(-1).astype(jnp.int32)
    new_features = relocate(stepped, target_pos)
    new_first = relocate(first_new, target_pos)
    new_second = relocate(second_new, target_pos)
    moved_positions = relocate(positions, target_pos)
    moved_scales = relocate(scales, target_pos)
    moved_opacity = relocate(opacity, target_pos)
    screen_second = view_screen(moved_positions, moved_scales, moved_opacity, cameras_second)
    colors_second = new_features.astype(jnp.bfloat16).reshape(N_VIEW, ROW_BINS, C, GB)
    image_second = lax.map(picture_of_view, (screen_second, colors_second, lists_second, loads_second, shift_second))
    return (image_second, new_features, new_first, new_second)
```

```python
import functools

import jax
import jax.numpy as jnp
from jax import lax
from jax.experimental import pallas as pl
from jax.experimental.pallas import tpu as pltpu
from jax.sharding import PartitionSpec as P

C = 64
GB = 128
PIX = 256
SIDE = 16
LBLK = 8
TILES = 16
BINS = 8
N_VIEW = 8
N_TILE = 32
ROWS = GB // 8
PACK = 3 * C + 8

beta_first = 0.9
beta_second = 0.999
learn_rate = 0.05
adam_epsilon = 1e-08
bias_first = 1.0 - 0.9**10
bias_second = 1.0 - 0.999**10

VM = pl.BlockSpec(memory_space=pltpu.VMEM)
SM = pl.BlockSpec(memory_space=pltpu.SMEM)
f32 = jnp.float32
bf16 = jnp.bfloat16


def params(mib, **more):
    return pltpu.CompilerParams(vmem_limit_bytes=mib * 1024 * 1024, **more)


def onehot(inverse):
    row = lax.broadcasted_iota(jnp.int32, (GB, GB), 0)
    col = lax.broadcasted_iota(jnp.int32, (GB, GB), 1)
    if inverse:
        row, col = col, row
    return jnp.where(col == (row % ROWS) * 8 + row // ROWS, 1.0, 0.0).astype(bf16)


def reorder(values, inverse):
    return jnp.dot(values, onehot(inverse), preferred_element_type=f32)


def reorder_wide(values, inverse):
    high = values.astype(bf16)
    rest = values - high.astype(f32)
    middle = rest.astype(bf16)
    low = (rest - middle.astype(f32)).astype(bf16)
    return (reorder(high, inverse) + reorder(middle, inverse)) + reorder(low, inverse)


def project_rows(p0, p1, p2, scales, opacity, camera):
    mean_x = camera[0, 0] * p0 + camera[0, 1] * p1 + camera[0, 2] * p2 + camera[0, 3]
    mean_y = camera[1, 0] * p0 + camera[1, 1] * p1 + camera[1, 2] * p2 + camera[1, 3]
    falloff = 0.5 / (scales * scales)
    opaque = 1.0 / (1.0 + jnp.exp(-opacity))
    stack = jnp.concatenate([mean_x, mean_y, falloff, opaque], axis=0)
    return reorder(stack.astype(bf16), False)


def spread(stack, screen_ref):
    for b in range(BINS):
        for k in range(4):
            screen_ref[0, b, k, :] = stack[k * BINS + b]
        screen_ref[0, b, 4:, :] = jnp.zeros((4, GB), f32)
    first = screen_ref[0]
    for t in range(1, N_TILE):
        screen_ref[t] = first


def prep_kernel(camera, owner, feat, m1, m2, pos, scales, opacity, colors, screen, packed):
    flat = feat[...].reshape(BINS * C, GB).astype(bf16)
    colors[...] = reorder(flat, False).astype(bf16).reshape(BINS, C, GB)
    stack = project_rows(pos[:, 0, :], pos[:, 1, :], pos[:, 2, :], scales[...], opacity[...], camera)
    spread(stack, screen)
    for s in range(BINS):
        w = owner[s]
        packed[w, 0:C] = feat[s]
        packed[w, C : 2 * C] = m1[s]
        packed[w, 2 * C : 3 * C] = m2[s]
        packed[w, 3 * C : 3 * C + 3] = pos[s]
        packed[w, 3 * C + 3 : 3 * C + 4] = scales[s : s + 1]
        packed[w, 3 * C + 4 : 3 * C + 5] = opacity[s : s + 1]
        packed[w, 3 * C + 5 :] = jnp.zeros((3, GB), f32)


def prep(camera, owner, feat, m1, m2, pos, scales, opacity):
    return pl.pallas_call(
        prep_kernel,
        out_shape=(
            jax.ShapeDtypeStruct((BINS, C, GB), bf16),
            jax.ShapeDtypeStruct((N_TILE, BINS, 8, GB), f32),
            jax.ShapeDtypeStruct((N_VIEW, PACK, GB), f32),
        ),
        in_specs=[SM, SM] + [VM] * 6,
        out_specs=(VM, VM, VM),
        compiler_params=params(16),
        name="prep",
    )(camera, owner, feat, m1, m2, pos, scales, opacity)


def screen_kernel(camera, geometry, screen):
    rows = [jnp.concatenate([geometry[b, k : k + 1] for b in range(BINS)], axis=0) for k in range(5)]
    spread(project_rows(*rows, camera), screen)


def screen_again(camera, geometry):
    return pl.pallas_call(
        screen_kernel,
        out_shape=jax.ShapeDtypeStruct((N_TILE, BINS, 8, GB), f32),
        in_specs=[SM, VM],
        out_specs=VM,
        compiler_params=params(16),
        name="screen_again",
    )(camera, geometry)


def weights_kernel(lists, loads, shift, screen, out):
    tile = pl.program_id(0)
    live = loads[tile]
    pixel = lax.broadcasted_iota(jnp.int32, (1, PIX), 1)
    place_x = (pixel % SIDE).astype(f32) + 0.5 + shift[tile, 0]
    place_y = (pixel // SIDE).astype(f32) + 0.5 + shift[tile, 1]
    row = lax.broadcasted_iota(jnp.int32, (8, PIX), 0)

    def block(q, carried):
        columns = screen[lists[tile, q]].T
        delta_x = place_x - columns[:, 0:1]
        delta_y = place_y - columns[:, 1:2]
        alphas = columns[:, 3:4] * jnp.exp(-columns[:, 2:3] * (delta_x * delta_x + delta_y * delta_y))
        keep = 1.0 - alphas
        running = jnp.ones((8, PIX), f32)
        parts = []
        for v in range(ROWS):
            parts.append(alphas[v * 8 : v * 8 + 8] * running)
            running = running * keep[v * 8 : v * 8 + 8]
        total = running
        for step in (1, 2, 4):
            total = total * jnp.where(row >= step, pltpu.roll(total, step, 0), 1.0)
        before = carried * jnp.where(row >= 1, pltpu.roll(total, 1, 0), 1.0)
        out[0, q] = jnp.concatenate([part * before for part in parts], axis=0).astype(bf16)
        return carried * jnp.broadcast_to(total[7:8], (8, PIX))

    lax.fori_loop(0, live, block, jnp.ones((8, PIX), f32))

    def dead(q, unused):
        out[0, q] = jnp.zeros((GB, PIX), bf16)
        return unused

    lax.fori_loop(live, LBLK, dead, 0)


def weights(lists, loads, shift, screen, name):
    return pl.pallas_call(
        weights_kernel,
        out_shape=jax.ShapeDtypeStruct((TILES, LBLK, GB, PIX), bf16),
        grid=(TILES,),
        in_specs=[SM, SM, SM, VM],
        out_specs=pl.BlockSpec((1, LBLK, GB, PIX), lambda i: (i, 0, 0, 0)),
        compiler_params=params(12),
        cost_estimate=pl.CostEstimate(
            flops=TILES * LBLK * GB * PIX * 14, bytes_accessed=10_000_000, transcendentals=TILES * LBLK * GB * PIX
        ),
        name=name,
    )(lists, loads, shift, screen.reshape(N_TILE * BINS, 8, GB))


def load_colors(blocks, colors, sems):
    @pl.when(pl.program_id(0) == 0)
    def _():
        copies = [
            pltpu.make_async_copy(block, colors.at[pl.ds(i * 32, 32)], sems.at[i]) for i, block in enumerate(blocks)
        ]
        for copy in copies:
            copy.start()
        for copy in copies:
            copy.wait()


def picture(slots, tile, w_ref, colors):
    row = jnp.concatenate([colors[slots[tile, q]] for q in range(LBLK)], axis=1)
    return jnp.dot(row, w_ref[0].reshape(LBLK * GB, PIX), preferred_element_type=f32)


def first_kernel(slots, w_ref, target, *rest):
    blocks, (own, other), (colors, total, sems, out_sems) = rest[:8], rest[8:10], rest[10:]
    tile = pl.program_id(0)

    @pl.when(tile == 0)
    def _():
        def clear(i, unused):
            total[i] = jnp.zeros((C, GB), f32)
            return unused

        lax.fori_loop(0, N_TILE * BINS, clear, 0)

    load_colors(blocks, colors, sems)
    residual = (picture(slots, tile, w_ref, colors) - target[0].astype(f32)).astype(bf16)
    pieces = lax.dot_general(
        residual, w_ref[0].reshape(LBLK * GB, PIX), (((1,), (1,)), ((), ())), preferred_element_type=f32
    )
    for q in range(LBLK):
        slot = slots[tile, q]
        total[slot] = total[slot] + pieces[:, q * GB : q * GB + GB]

    @pl.when(tile == TILES - 1)
    def _():
        half = N_TILE * BINS // 2
        copies = [
            pltpu.make_async_copy(total.at[pl.ds(half, half)], other, out_sems.at[0]),
            pltpu.make_async_copy(total.at[pl.ds(0, half)], own, out_sems.at[1]),
        ]
        for copy in copies:
            copy.start()
        for copy in copies:
            copy.wait()


ANY = pl.BlockSpec(memory_space=pl.ANY)


def first_render(slots, w, target, blocks):
    half = N_TILE * BINS // 2
    return pl.pallas_call(
        first_kernel,
        out_shape=(jax.ShapeDtypeStruct((half, C, GB), f32),) * 2,
        grid=(TILES,),
        in_specs=[
            SM,
            pl.BlockSpec((1, LBLK, GB, PIX), lambda i: (i, 0, 0, 0)),
            pl.BlockSpec((1, C, PIX), lambda i: (i, 0, 0)),
        ]
        + [ANY] * 8,
        out_specs=(ANY, ANY),
        scratch_shapes=[
            pltpu.VMEM((N_TILE * BINS, C, GB), bf16),
            pltpu.VMEM((N_TILE * BINS, C, GB), f32),
            pltpu.SemaphoreType.DMA((8,)),
            pltpu.SemaphoreType.DMA((2,)),
        ],
        compiler_params=params(24),
        cost_estimate=pl.CostEstimate(flops=TILES * LBLK * C * GB * PIX * 4, bytes_accessed=25_000_000, transcendentals=0),
        name="first_render",
    )(slots, w, target, *blocks)


def second_kernel(slots, w_ref, *rest):
    blocks, image, (colors, sems) = rest[:8], rest[8], rest[9:]
    load_colors(blocks, colors, sems)
    image[0] = picture(slots, pl.program_id(0), w_ref, colors)


def second_render(slots, w, blocks):
    return pl.pallas_call(
        second_kernel,
        out_shape=jax.ShapeDtypeStruct((TILES, C, PIX), f32),
        grid=(TILES,),
        in_specs=[SM, pl.BlockSpec((1, LBLK, GB, PIX), lambda i: (i, 0, 0, 0))] + [ANY] * 8,
        out_specs=pl.BlockSpec((1, C, PIX), lambda i: (i, 0, 0)),
        scratch_shapes=[pltpu.VMEM((N_TILE * BINS, C, GB), bf16), pltpu.SemaphoreType.DMA((8,))],
        compiler_params=params(16),
        cost_estimate=pl.CostEstimate(flops=TILES * LBLK * C * GB * PIX * 2, bytes_accessed=14_000_000, transcendentals=0),
        name="second_render",
    )(slots, w, *blocks)


def adam_kernel(gradient, packed, feat, first, second, colors):
    g = reorder_wide(gradient[...].reshape(BINS * C, GB), True).reshape(BINS, C, GB)
    first_new = beta_first * packed[:, C : 2 * C] + (1.0 - beta_first) * g
    second_new = beta_second * packed[:, 2 * C : 3 * C] + (1.0 - beta_second) * g * g
    stepped = packed[:, 0:C] - learn_rate * (first_new / bias_first) / (
        jnp.sqrt(second_new / bias_second) + adam_epsilon
    )
    first[...] = first_new
    second[...] = second_new
    feat[...] = stepped
    flat = stepped.reshape(BINS * C, GB).astype(bf16)
    colors[...] = reorder(flat, False).astype(bf16).reshape(BINS, C, GB)


def adam(gradient, packed):
    wide = jax.ShapeDtypeStruct((BINS, C, GB), f32)
    return pl.pallas_call(
        adam_kernel,
        out_shape=(wide, wide, wide, jax.ShapeDtypeStruct((BINS, C, GB), bf16)),
        in_specs=[VM, VM],
        out_specs=(VM,) * 4,
        compiler_params=params(16),
        name="adam",
    )(gradient, packed)


def device(x, y, c):
    return ((x % 4) * 4 + y % 4) * 2 + c


def shift_by(value, level, k):
    pairs = []
    for x in range(4):
        for y in range(4):
            for c in range(2):
                dx, dy = (k, 0) if c == level else (0, k)
                pairs.append((device(x, y, c), device(x + dx, y + dy, c)))
    return lax.ppermute(value, "tile", pairs)


def swap_core(value):
    pairs = [(t, t ^ 1) for t in range(N_TILE)]
    return lax.ppermute(value, "tile", pairs)


ORDER = (2, 1, 3)


def gather_colors(colors):
    near = {0: colors}
    for k in ORDER:
        near[k] = shift_by(colors, 0, k)
    line = jnp.concatenate([near[k] for k in range(4)], axis=0)
    plane = {0: line}
    for k in ORDER:
        plane[k] = shift_by(line, 1, k)
    own = [plane[k] for k in range(4)]
    return own + [swap_core(block) for block in own]


def scatter_grads(own, other):
    half16 = jnp.float16
    size = 4 * BINS
    summed = {}
    for k in ORDER + (0,):
        got = swap_core(other[k * size : (k + 1) * size].astype(half16))
        summed[k] = own[k * size : (k + 1) * size] + got.astype(f32)
    line = summed[0]
    for k in ORDER:
        line = line + shift_by(summed[k].astype(half16), 1, -k).astype(f32)
    total = line[0:BINS]
    for k in ORDER:
        total = total + shift_by(line[k * BINS : (k + 1) * BINS].astype(half16), 0, -k).astype(f32)
    return total


def color_slots(lists):
    me = lax.axis_index("tile")
    x, y, c = me // 8, (me // 2) % 4, me % 2
    owner, within = lists // BINS, lists % BINS
    far_x = (x - owner // 8) % 4
    far_y = (y - (owner // 2) % 4) % 4
    core = owner % 2
    near = jnp.where(core == 0, far_x, far_y)
    far = jnp.where(core == 0, far_y, far_x)
    return (((core ^ c) * 4 + far) * 4 + near) * BINS + within


def across_view(value):
    return lax.all_to_all(value, "view", split_axis=0, concat_axis=0, tiled=True)


def across_tile(value):
    return lax.all_to_all(value, "tile", split_axis=0, concat_axis=0, tiled=True)


def local(
    features,
    moment_first,
    moment_second,
    positions,
    scales,
    opacity,
    cameras_first,
    shift_first,
    lists_first,
    loads_first,
    target,
    owner_after,
    cameras_second,
    shift_second,
    lists_second,
    loads_second,
):
    colors, screen, packed = prep(
        cameras_first[0], owner_after, features, moment_first, moment_second, positions, scales, opacity
    )
    screen = across_tile(screen)
    blocks = gather_colors(colors)
    w_first = weights(lists_first[0], loads_first[0], shift_first[0], screen, "weights_first")
    moved = across_view(packed)
    screen_next = across_tile(screen_again(cameras_second[0], moved[:, 3 * C :]))
    own, other = first_render(color_slots(lists_first[0]), w_first, target[0], blocks)
    w_second = weights(lists_second[0], loads_second[0], shift_second[0], screen_next, "weights_second")
    gradient = scatter_grads(own, other)
    ordering = jnp.argsort(owner_after, stable=True)
    gradient = across_view(gradient[ordering].astype(jnp.float16)).astype(f32)
    new_features, new_first, new_second, colors_next = adam(gradient, moved)
    blocks_next = gather_colors(colors_next)
    image = second_render(color_slots(lists_second[0]), w_second, blocks_next)
    return (image[None], new_features, new_first, new_second)


def solution(mesh):
    return jax.shard_map(
        local,
        mesh=mesh,
        in_specs=(
            P(("view", "tile"), None, None),
            P(("view", "tile"), None, None),
            P(("view", "tile"), None, None),
            P(("view", "tile"), None, None),
            P(("view", "tile"), None),
            P(("view", "tile"), None),
            P("view", None, None),
            P("view", "tile", None),
            P("view", "tile", None),
            P("view", "tile"),
            P("view", "tile", None, None),
            P(("view", "tile")),
            P("view", None, None),
            P("view", "tile", None),
            P("view", "tile", None),
            P("view", "tile"),
        ),
        out_specs=(
            P("view", "tile", None, None),
            P(("view", "tile"), None, None),
            P(("view", "tile"), None, None),
            P(("view", "tile"), None, None),
        ),
        check_vma=False,
    )
```

```python
import functools

import jax
import jax.numpy as jnp
from jax import lax
from jax.experimental import pallas as pl
from jax.experimental.pallas import tpu as pltpu
from jax.sharding import PartitionSpec as P

C = 64
GB = 128
PIX = 256
SIDE = 16
LBLK = 8
TILES = 16
BINS = 8
N_VIEW = 8
N_TILE = 32
ROWS = GB // 8
PACK = 3 * C + 8

beta_first = 0.9
beta_second = 0.999
learn_rate = 0.05
adam_epsilon = 1e-08
bias_first = 1.0 - 0.9**10
bias_second = 1.0 - 0.999**10

VM = pl.BlockSpec(memory_space=pltpu.VMEM)
SM = pl.BlockSpec(memory_space=pltpu.SMEM)
ANY = pl.BlockSpec(memory_space=pl.ANY)
WEIGHTS_MIB = 56
RENDER_MIB = 44
LOG2E = 1.4426950408889634
f32 = jnp.float32
bf16 = jnp.bfloat16


def params(mib, **more):
    return pltpu.CompilerParams(vmem_limit_bytes=mib * 1024 * 1024, **more)


def onehot(inverse):
    row = lax.broadcasted_iota(jnp.int32, (GB, GB), 0)
    col = lax.broadcasted_iota(jnp.int32, (GB, GB), 1)
    if inverse:
        row, col = col, row
    return jnp.where(col == (row % ROWS) * 8 + row // ROWS, 1.0, 0.0).astype(bf16)


def reorder(values, inverse):
    return jnp.dot(values, onehot(inverse), preferred_element_type=f32)


def reorder_wide(values, inverse):
    high = values.astype(bf16)
    rest = values - high.astype(f32)
    middle = rest.astype(bf16)
    low = (rest - middle.astype(f32)).astype(bf16)
    return (reorder(high, inverse) + reorder(middle, inverse)) + reorder(low, inverse)


def project_rows(p0, p1, p2, scales, opacity, camera):
    mean_x = camera[0, 0] * p0 + camera[0, 1] * p1 + camera[0, 2] * p2 + camera[0, 3]
    mean_y = camera[1, 0] * p0 + camera[1, 1] * p1 + camera[1, 2] * p2 + camera[1, 3]
    falloff = 0.5 / (scales * scales)
    opaque = 1.0 / (1.0 + jnp.exp(-opacity))
    stack = jnp.concatenate([mean_x, mean_y, falloff, opaque], axis=0)
    return reorder(stack.astype(bf16), False)


def screen_rows(stack):
    rows = [stack[k * BINS + b : k * BINS + b + 1] for b in range(BINS) for k in range(4)]
    return jnp.concatenate(rows, axis=0).astype(bf16)


def spread(stack, screen):
    rows = screen_rows(stack)
    for t in range(N_TILE):
        screen[t] = rows


def fetch(pairs, sems):
    copies = [pltpu.make_async_copy(source, to, sems.at[i]) for i, (source, to) in enumerate(pairs)]
    for copy in copies:
        copy.start()
    return copies


def prep_kernel(camera_hbm, feat_hbm, pos_hbm, scales_hbm, opacity_hbm, colors, screen, *scratch):
    camera, feat, pos, scales, opacity, sems = scratch
    copies = fetch(
        [(camera_hbm, camera), (feat_hbm, feat), (pos_hbm, pos), (scales_hbm, scales), (opacity_hbm, opacity)], sems
    )
    for copy in copies:
        copy.wait()
    flat = feat[...].reshape(BINS * C, GB).astype(bf16)
    colors[...] = reorder(flat, False).astype(bf16).reshape(BINS, C, GB)
    stack = project_rows(pos[0], pos[1], pos[2], scales[...], opacity[...], camera.at[0])
    spread(stack, screen)


def prep(camera, feat, pos, scales, opacity):
    return pl.pallas_call(
        prep_kernel,
        out_shape=(
            jax.ShapeDtypeStruct((BINS, C, GB), bf16),
            jax.ShapeDtypeStruct((N_TILE, BINS * 4, GB), bf16),
        ),
        in_specs=[ANY] * 5,
        out_specs=(VM, VM),
        scratch_shapes=[
            pltpu.SMEM((1, 2, 4), f32),
            pltpu.VMEM((BINS, C, GB), f32),
            pltpu.VMEM((3, BINS, GB), f32),
            pltpu.VMEM((BINS, GB), f32),
            pltpu.VMEM((BINS, GB), f32),
            pltpu.SemaphoreType.DMA((5,)),
        ],
        compiler_params=params(60),
        name="prep",
    )(camera, feat, pos, scales, opacity)


def pack_kernel(owner, feat_hbm, m1_hbm, m2_hbm, pos_hbm, scales_hbm, opacity_hbm, packed, *scratch):
    feat, m1, m2, pos, scales, opacity, sems = scratch
    copies = fetch(
        [
            (feat_hbm, feat),
            (m1_hbm, m1),
            (m2_hbm, m2),
            (pos_hbm, pos),
            (scales_hbm, scales),
            (opacity_hbm, opacity),
        ],
        sems,
    )
    for copy in copies:
        copy.wait()
    for s in range(BINS):
        w = owner[s]
        packed[w, 0:C] = feat[s]
        packed[w, C : 2 * C] = m1[s]
        packed[w, 2 * C : 3 * C] = m2[s]
        for k in range(3):
            packed[w, 3 * C + k : 3 * C + k + 1] = pos[k, s : s + 1]
        packed[w, 3 * C + 3 : 3 * C + 4] = scales[s : s + 1]
        packed[w, 3 * C + 4 : 3 * C + 5] = opacity[s : s + 1]
        packed[w, 3 * C + 5 :] = jnp.zeros((3, GB), f32)


def pack(owner, feat, m1, m2, pos, scales, opacity):
    return pl.pallas_call(
        pack_kernel,
        out_shape=jax.ShapeDtypeStruct((N_VIEW, PACK, GB), f32),
        in_specs=[SM] + [ANY] * 6,
        out_specs=VM,
        scratch_shapes=[pltpu.VMEM((BINS, C, GB), f32)] * 3
        + [
            pltpu.VMEM((3, BINS, GB), f32),
            pltpu.VMEM((BINS, GB), f32),
            pltpu.VMEM((BINS, GB), f32),
            pltpu.SemaphoreType.DMA((6,)),
        ],
        compiler_params=params(56),
        name="pack",
    )(owner, feat, m1, m2, pos, scales, opacity)


def screen_kernel(camera, geometry, screen):
    rows = [jnp.concatenate([geometry[b, k : k + 1] for b in range(BINS)], axis=0) for k in range(5)]
    spread(project_rows(*rows, camera), screen)


def screen_again(camera, geometry):
    return pl.pallas_call(
        screen_kernel,
        out_shape=jax.ShapeDtypeStruct((N_TILE, BINS * 4, GB), bf16),
        in_specs=[SM, VM],
        out_specs=VM,
        compiler_params=params(8),
        name="screen_again",
    )(camera, geometry)


def weights_kernel(lists, loads, shift, screen, out_hbm, token, bins, out, sems):
    token[...] = jnp.zeros((8, GB), f32)
    row = lax.broadcasted_iota(jnp.int32, (8, GB), 0)
    factor = jnp.where(row % 4 == 2, -LOG2E, 1.0)

    def widen(t, unused):
        rows = screen[t].astype(f32)
        for i in range(BINS // 2):
            two = rows[8 * i : 8 * i + 8] * factor
            bins[t * BINS + 2 * i] = two
            bins[t * BINS + 2 * i + 1] = pltpu.roll(two, 4, 0)
        return unused

    lax.fori_loop(0, N_TILE, widen, 0)
    lane = lax.broadcasted_iota(jnp.int32, (8, GB), 1)
    pixel_x = (lane % SIDE).astype(f32) + 0.5
    pixel_y = (lane // SIDE).astype(f32) + 0.5

    def one(tile, q, live, place_x, place_y):
        values = bins[lists[tile, q]]
        alive = jnp.where(q < live, 1.0, 0.0)
        columns = jnp.where(row == 3, values * alive, values).T
        running = [jnp.ones((8, GB), f32) for half in range(2)]
        parts = [[], []]
        for v in range(ROWS):
            some = columns[v * 8 : v * 8 + 8]
            mean_x, mean_y, fall, opaque = (jnp.broadcast_to(some[:, k : k + 1], (8, GB)) for k in range(4))
            delta_x = place_x - mean_x
            along_x = delta_x * delta_x * fall
            for half in range(2):
                delta_y = place_y[half] - mean_y
                part = opaque * jnp.exp2(along_x + delta_y * delta_y * fall) * running[half]
                parts[half].append(part)
                running[half] = running[half] - part
        before, after = [], []
        for total in running:
            for step in (1, 2, 4):
                total = total * jnp.where(row >= step, pltpu.roll(total, step, 0), 1.0)
            before.append(jnp.where(row >= 1, pltpu.roll(total, 1, 0), 1.0))
            after.append(jnp.broadcast_to(total[7:8], (8, GB)))
        return parts, before, after

    def store(slot, q, parts, before):
        for half in range(2):
            rows = [part * before[half] for part in parts[half]]
            out[slot, q, :, half * GB : half * GB + GB] = jnp.concatenate(rows, axis=0).astype(bf16)

    def leave(tile):
        slot = tile % 2
        return pltpu.make_async_copy(out.at[slot], out_hbm.at[tile], sems.at[slot])

    def each_tile(tile, unused):
        live = loads[tile]
        slot = tile % 2

        @pl.when(tile >= 2)
        def _():
            leave(tile - 2).wait()

        place_x = pixel_x + shift[tile, 0]
        place_y = [pixel_y + shift[tile, 1] + 8.0 * half for half in range(2)]

        def pair(j, carried):
            first = one(tile, 2 * j, live, place_x, place_y)
            second = one(tile, 2 * j + 1, live, place_x, place_y)
            store(slot, 2 * j, first[0], [carried[h] * first[1][h] for h in range(2)])
            middle = [carried[h] * first[2][h] for h in range(2)]
            store(slot, 2 * j + 1, second[0], [middle[h] * second[1][h] for h in range(2)])
            return tuple(middle[h] * second[2][h] for h in range(2))

        pairs = (live + 1) // 2
        lax.fori_loop(0, pairs, pair, (jnp.ones((8, GB), f32),) * 2)

        def dead(q, unused):
            out[slot, q] = jnp.zeros((GB, PIX), bf16)
            return unused

        lax.fori_loop(2 * pairs, LBLK, dead, 0)
        leave(tile).start()
        return unused

    lax.fori_loop(0, TILES, each_tile, 0)
    leave(TILES - 2).wait()
    leave(TILES - 1).wait()


def weights(lists, loads, shift, screen, name):
    return pl.pallas_call(
        weights_kernel,
        out_shape=(jax.ShapeDtypeStruct((TILES, LBLK, GB, PIX), bf16), jax.ShapeDtypeStruct((8, GB), f32)),
        in_specs=[SM, SM, SM, VM],
        out_specs=(ANY, VM),
        scratch_shapes=[
            pltpu.VMEM((N_TILE * BINS, 8, GB), f32),
            pltpu.VMEM((2, LBLK, GB, PIX), bf16),
            pltpu.SemaphoreType.DMA((2,)),
        ],
        compiler_params=params(WEIGHTS_MIB),
        cost_estimate=pl.CostEstimate(
            flops=TILES * LBLK * GB * PIX * 14, bytes_accessed=10_000_000, transcendentals=TILES * LBLK * GB * PIX
        ),
        name=name,
    )(lists, loads, shift, screen)


def load_colors(blocks, colors, sems):
    return fetch([(block, colors.at[pl.ds(i * 32, 32)]) for i, block in enumerate(blocks)], sems)


def fetch_weights(w_hbm, w, sems, tile):
    slot = tile % 2
    return pltpu.make_async_copy(w_hbm.at[tile], w.at[slot], sems.at[slot])


def over_tiles(w_hbm, w, sems, body):
    def each_tile(tile, unused):
        @pl.when(tile + 1 < TILES)
        def _():
            fetch_weights(w_hbm, w, sems, tile + 1).start()

        fetch_weights(w_hbm, w, sems, tile).wait()
        body(tile, w[tile % 2].reshape(LBLK * GB, PIX))
        return unused

    lax.fori_loop(0, TILES, each_tile, 0)


def picture(slots, tile, w, colors):
    row = jnp.concatenate([colors[slots[tile, q]] for q in range(LBLK)], axis=1)
    return jnp.dot(row, w, preferred_element_type=f32)


def first_kernel(slots, token, w_hbm, target_hbm, *rest):
    blocks, total, (colors, w, target, sems, w_sems, t_sem) = rest[:8], rest[8], rest[9:]
    fetch_weights(w_hbm, w, w_sems, 0).start()
    copies = load_colors(blocks, colors, sems) + fetch([(target_hbm, target)], t_sem)

    def clear(i, unused):
        total[pl.ds(i * 8, 8)] = jnp.zeros((8, C, GB), f32)
        return unused

    lax.fori_loop(0, N_TILE, clear, 0)
    for copy in copies:
        copy.wait()

    def body(tile, w):
        residual = (picture(slots, tile, w, colors) - target[tile].astype(f32)).astype(bf16)
        pieces = lax.dot_general(residual, w, (((1,), (1,)), ((), ())), preferred_element_type=f32)
        for q in range(LBLK):
            slot = slots[tile, q]
            total[slot] = total[slot] + pieces[:, q * GB : q * GB + GB]

    over_tiles(w_hbm, w, w_sems, body)


def first_render(slots, token, w, target, blocks):
    return pl.pallas_call(
        first_kernel,
        out_shape=jax.ShapeDtypeStruct((N_TILE * BINS, C, GB), f32),
        in_specs=[SM, ANY, ANY, ANY] + [ANY] * 8,
        out_specs=VM,
        scratch_shapes=[
            pltpu.VMEM((N_TILE * BINS, C, GB), bf16),
            pltpu.VMEM((2, LBLK, GB, PIX), bf16),
            pltpu.VMEM((TILES, C, PIX), bf16),
            pltpu.SemaphoreType.DMA((8,)),
            pltpu.SemaphoreType.DMA((2,)),
            pltpu.SemaphoreType.DMA((1,)),
        ],
        compiler_params=params(RENDER_MIB),
        cost_estimate=pl.CostEstimate(flops=TILES * LBLK * C * GB * PIX * 4, bytes_accessed=25_000_000, transcendentals=0),
        name="first_render",
    )(slots, token, w, target, *blocks)


def second_kernel(slots, token, w_hbm, *rest):
    blocks, image, (colors, w, sems, w_sems) = rest[:8], rest[8], rest[9:]
    fetch_weights(w_hbm, w, w_sems, 0).start()
    for copy in load_colors(blocks, colors, sems):
        copy.wait()

    def body(tile, w):
        image[tile] = picture(slots, tile, w, colors)

    over_tiles(w_hbm, w, w_sems, body)


def second_render(slots, token, w, blocks):
    return pl.pallas_call(
        second_kernel,
        out_shape=jax.ShapeDtypeStruct((TILES, C, PIX), f32),
        in_specs=[SM, ANY, ANY] + [ANY] * 8,
        out_specs=VM,
        scratch_shapes=[
            pltpu.VMEM((N_TILE * BINS, C, GB), bf16),
            pltpu.VMEM((2, LBLK, GB, PIX), bf16),
            pltpu.SemaphoreType.DMA((8,)),
            pltpu.SemaphoreType.DMA((2,)),
        ],
        compiler_params=params(RENDER_MIB),
        cost_estimate=pl.CostEstimate(flops=TILES * LBLK * C * GB * PIX * 2, bytes_accessed=14_000_000, transcendentals=0),
        name="second_render",
    )(slots, token, w, *blocks)


def adam_kernel(gradient, packed, feat, first, second, colors):
    g = reorder_wide(gradient[...].reshape(BINS * C, GB), True).reshape(BINS, C, GB)
    first_new = beta_first * packed[:, C : 2 * C] + (1.0 - beta_first) * g
    second_new = beta_second * packed[:, 2 * C : 3 * C] + (1.0 - beta_second) * g * g
    stepped = packed[:, 0:C] - learn_rate * (first_new / bias_first) / (
        jnp.sqrt(second_new / bias_second) + adam_epsilon
    )
    first[...] = first_new
    second[...] = second_new
    feat[...] = stepped
    flat = stepped.reshape(BINS * C, GB).astype(bf16)
    colors[...] = reorder(flat, False).astype(bf16).reshape(BINS, C, GB)


def adam(gradient, packed):
    wide = jax.ShapeDtypeStruct((BINS, C, GB), f32)
    return pl.pallas_call(
        adam_kernel,
        out_shape=(wide, wide, wide, jax.ShapeDtypeStruct((BINS, C, GB), bf16)),
        in_specs=[VM, VM],
        out_specs=(VM,) * 4,
        compiler_params=params(16),
        name="adam",
    )(gradient, packed)


def device(x, y, c):
    return ((x % 4) * 4 + y % 4) * 2 + c


def shift_by(value, level, k):
    pairs = []
    for x in range(4):
        for y in range(4):
            for c in range(2):
                dx, dy = (k, 0) if c == level else (0, k)
                pairs.append((device(x, y, c), device(x + dx, y + dy, c)))
    return lax.ppermute(value, "tile", pairs)


def swap_core(value):
    pairs = [(t, t ^ 1) for t in range(N_TILE)]
    return lax.ppermute(value, "tile", pairs)


ORDER = (2, 1, 3)


def tie(*values):
    return lax.optimization_barrier(values)


def gather_line(colors):
    near = {0: colors}
    for k in ORDER:
        near[k] = shift_by(colors, 0, k)
    return jnp.concatenate([near[k] for k in range(4)], axis=0)


def gather_plane(line):
    plane = {0: line}
    for k in ORDER:
        plane[k] = shift_by(line, 1, k)
    return [plane[k] for k in range(4)]


def swapped(own):
    return list(own) + [swap_core(block) for block in own]


def scatter_far(total):
    half16 = jnp.float16
    size = 4 * BINS
    other = N_TILE * BINS // 2
    summed = {}
    for k in ORDER + (0,):
        got = swap_core(total[other + k * size : other + (k + 1) * size].astype(half16))
        summed[k] = total[k * size : (k + 1) * size] + got.astype(f32)
    line = summed[0]
    for k in ORDER:
        line = line + shift_by(summed[k].astype(half16), 1, -k).astype(f32)
    return line


def scatter_near(line):
    half16 = jnp.float16
    total = line[0:BINS]
    for k in ORDER:
        total = total + shift_by(line[k * BINS : (k + 1) * BINS].astype(half16), 0, -k).astype(f32)
    return total


def color_slots(lists):
    me = lax.axis_index("tile")
    x, y, c = me // 8, (me // 2) % 4, me % 2
    owner, within = lists // BINS, lists % BINS
    far_x = (x - owner // 8) % 4
    far_y = (y - (owner // 2) % 4) % 4
    core = owner % 2
    near = jnp.where(core == 0, far_x, far_y)
    far = jnp.where(core == 0, far_y, far_x)
    return (((core ^ c) * 4 + far) * 4 + near) * BINS + within


def across_view(value):
    return lax.all_to_all(value, "view", split_axis=0, concat_axis=0, tiled=True)


def across_tile(value):
    return lax.all_to_all(value, "tile", split_axis=0, concat_axis=0, tiled=True)


def local(
    features,
    moment_first,
    moment_second,
    positions,
    scales,
    opacity,
    cameras_first,
    shift_first,
    lists_first,
    loads_first,
    target,
    owner_after,
    cameras_second,
    shift_second,
    lists_second,
    loads_second,
):
    positions = jnp.transpose(positions, (1, 0, 2))
    colors, screen = prep(cameras_first, features, positions, scales, opacity)
    packed = pack(owner_after, features, moment_first, moment_second, positions, scales, opacity)
    screen = across_tile(screen)
    line, packed = tie(gather_line(colors), packed)
    moved = across_view(packed)
    own = gather_plane(line)
    w_first, token = weights(lists_first[0], loads_first[0], shift_first[0], screen, "weights_first")
    *own, token = tie(*own, token)
    *blocks, moved = tie(*swapped(own), moved)
    total = first_render(color_slots(lists_first[0]), token, w_first, target[0], blocks)
    screen_next = across_tile(screen_again(cameras_second[0], moved[:, 3 * C :]))
    w_second, token = weights(lists_second[0], loads_second[0], shift_second[0], screen_next, "weights_second")
    line, token = tie(scatter_far(total), token)
    gradient = scatter_near(line)
    ordering = jnp.argsort(owner_after, stable=True)
    gradient = across_view(gradient[ordering].astype(jnp.float16)).astype(f32)
    new_features, new_first, new_second, colors_next = adam(gradient, moved)
    blocks_next = swapped(gather_plane(gather_line(colors_next)))
    image = second_render(color_slots(lists_second[0]), token, w_second, blocks_next)
    return (image[None], new_features, new_first, new_second)


def solution(mesh):
    return jax.shard_map(
        local,
        mesh=mesh,
        in_specs=(
            P(("view", "tile"), None, None),
            P(("view", "tile"), None, None),
            P(("view", "tile"), None, None),
            P(("view", "tile"), None, None),
            P(("view", "tile"), None),
            P(("view", "tile"), None),
            P("view", None, None),
            P("view", "tile", None),
            P("view", "tile", None),
            P("view", "tile"),
            P("view", "tile", None, None),
            P(("view", "tile")),
            P("view", None, None),
            P("view", "tile", None),
            P("view", "tile", None),
            P("view", "tile"),
        ),
        out_specs=(
            P("view", "tile", None, None),
            P(("view", "tile"), None, None),
            P(("view", "tile"), None, None),
            P(("view", "tile"), None, None),
        ),
        check_vma=False,
    )
```

```python
import functools

import jax
import jax.numpy as jnp
from jax import lax
from jax.experimental import pallas as pl
from jax.experimental.pallas import tpu as pltpu
from jax.sharding import PartitionSpec as P

C = 64
GB = 128
PIX = 256
SIDE = 16
LBLK = 8
TILES = 16
BINS = 8
N_VIEW = 8
N_TILE = 32
ROWS = GB // 8

beta_first = 0.9
beta_second = 0.999
learn_rate = 0.05
adam_epsilon = 1e-08
bias_first = 1.0 - 0.9**10
bias_second = 1.0 - 0.999**10

VM = pl.BlockSpec(memory_space=pltpu.VMEM)
SM = pl.BlockSpec(memory_space=pltpu.SMEM)
ANY = pl.BlockSpec(memory_space=pl.ANY)
GROUP = 8
WEIGHTS_MIB = 60
RENDER_MIB = 60
LOG2E = 1.4426950408889634
f32 = jnp.float32
bf16 = jnp.bfloat16


def params(mib, **more):
    return pltpu.CompilerParams(vmem_limit_bytes=mib * 1024 * 1024, **more)


def onehot(inverse):
    row = lax.broadcasted_iota(jnp.int32, (GB, GB), 0)
    col = lax.broadcasted_iota(jnp.int32, (GB, GB), 1)
    if inverse:
        row, col = col, row
    return jnp.where(col == (row % ROWS) * 8 + row // ROWS, 1.0, 0.0).astype(bf16)


def reorder(values, inverse):
    return jnp.dot(values, onehot(inverse), preferred_element_type=f32)


def reorder_wide(values, inverse):
    high = values.astype(bf16)
    rest = values - high.astype(f32)
    middle = rest.astype(bf16)
    low = (rest - middle.astype(f32)).astype(bf16)
    return (reorder(high, inverse) + reorder(middle, inverse)) + reorder(low, inverse)


def project_rows(p0, p1, p2, scales, opacity, camera):
    mean_x = camera[0, 0] * p0 + camera[0, 1] * p1 + camera[0, 2] * p2 + camera[0, 3]
    mean_y = camera[1, 0] * p0 + camera[1, 1] * p1 + camera[1, 2] * p2 + camera[1, 3]
    falloff = 0.5 / (scales * scales)
    opaque = 1.0 / (1.0 + jnp.exp(-opacity))
    stack = jnp.concatenate([mean_x, mean_y, falloff, opaque], axis=0)
    return reorder(stack.astype(bf16), False)


def screen_rows(stack):
    rows = [stack[k * BINS + b : k * BINS + b + 1] for b in range(BINS) for k in range(4)]
    return jnp.concatenate(rows, axis=0).astype(bf16)


def spread(stack, screen):
    rows = screen_rows(stack)
    for t in range(N_TILE):
        screen[t] = rows


def fetch(pairs, sems):
    copies = [pltpu.make_async_copy(source, to, sems.at[i]) for i, (source, to) in enumerate(pairs)]
    for copy in copies:
        copy.start()
    return copies


def prep_kernel(camera_hbm, owner_hbm, feat_hbm, pos_hbm, scales_hbm, opacity_hbm, colors, screen, geometry, *scratch):
    camera, owner, feat, pos, scales, opacity, sems = scratch
    copies = fetch(
        [
            (camera_hbm, camera),
            (owner_hbm, owner),
            (feat_hbm, feat),
            (pos_hbm, pos),
            (scales_hbm, scales),
            (opacity_hbm, opacity),
        ],
        sems,
    )
    for copy in copies:
        copy.wait()
    flat = feat[...].reshape(BINS * C, GB).astype(bf16)
    colors[...] = reorder(flat, False).astype(bf16).reshape(BINS, C, GB)
    stack = project_rows(pos[0], pos[1], pos[2], scales[...], opacity[...], camera.at[0])
    spread(stack, screen)
    for s in range(BINS):
        rows = [pos[k, s : s + 1] for k in range(3)]
        rows += [scales[s : s + 1], opacity[s : s + 1], jnp.zeros((3, GB), f32)]
        geometry[owner[s]] = jnp.concatenate(rows, axis=0)


def prep(camera, owner, feat, pos, scales, opacity):
    return pl.pallas_call(
        prep_kernel,
        out_shape=(
            jax.ShapeDtypeStruct((BINS, C, GB), bf16),
            jax.ShapeDtypeStruct((N_TILE, BINS * 4, GB), bf16),
            jax.ShapeDtypeStruct((N_VIEW, 8, GB), f32),
        ),
        in_specs=[ANY] * 6,
        out_specs=(VM, VM, VM),
        scratch_shapes=[
            pltpu.SMEM((1, 2, 4), f32),
            pltpu.SMEM((BINS,), jnp.int32),
            pltpu.VMEM((BINS, C, GB), f32),
            pltpu.VMEM((3, BINS, GB), f32),
            pltpu.VMEM((BINS, GB), f32),
            pltpu.VMEM((BINS, GB), f32),
            pltpu.SemaphoreType.DMA((6,)),
        ],
        compiler_params=params(60),
        name="prep",
    )(camera, owner, feat, pos, scales, opacity)


def screen_kernel(camera, geometry, screen):
    rows = [jnp.concatenate([geometry[b, k : k + 1] for b in range(BINS)], axis=0) for k in range(5)]
    spread(project_rows(*rows, camera), screen)


def screen_again(camera, geometry):
    return pl.pallas_call(
        screen_kernel,
        out_shape=jax.ShapeDtypeStruct((N_TILE, BINS * 4, GB), bf16),
        in_specs=[SM, VM],
        out_specs=VM,
        compiler_params=params(8),
        name="screen_again",
    )(camera, geometry)


def weights_kernel(lists_hbm, loads_hbm, shift_hbm, screen_hbm, out_hbm, token, *scratch):
    lists, loads, shift, screen, bins, out, work, sem, sems = scratch
    copies = fetch([(lists_hbm, lists), (loads_hbm, loads), (shift_hbm, shift), (screen_hbm, screen)], sems)
    token[...] = jnp.zeros((8, GB), f32)
    row = lax.broadcasted_iota(jnp.int32, (8, GB), 0)
    lane = lax.broadcasted_iota(jnp.int32, (8, GB), 1)
    pixel_x = (lane % SIDE).astype(f32) + 0.5
    pixel_y = (lane // SIDE).astype(f32) + 0.5
    for copy in copies:
        copy.wait()

    def widen(t, unused):
        rows = screen[t].astype(f32)
        for i in range(BINS // 2):
            two = rows[8 * i : 8 * i + 8]
            bins[t * BINS + 2 * i] = two
            bins[t * BINS + 2 * i + 1] = pltpu.roll(two, 4, 0)
        return unused

    lax.fori_loop(0, N_TILE, widen, 0, unroll=4)
    source = lax.broadcasted_iota(jnp.int32, (GROUP * 8, 4 * GB), 0)
    wanted = lax.broadcasted_iota(jnp.int32, (GROUP * 8, 4 * GB), 1) // GB

    def one(wide, place_x, place_y):
        running = [jnp.ones((8, GB), f32) for half in range(2)]
        parts = [[], []]
        for v in range(ROWS):
            some = wide[v * 8 : v * 8 + 8]
            mean_x, mean_y, fall, opaque = (some[:, k * GB : k * GB + GB] for k in range(4))
            fall = fall * -LOG2E
            delta_x = place_x - mean_x
            along_x = delta_x * delta_x * fall
            for half in range(2):
                delta_y = place_y[half] - mean_y
                part = opaque * jnp.exp2(along_x + delta_y * delta_y * fall) * running[half]
                parts[half].append(part)
                running[half] = running[half] - part
        before, after = [], []
        for total in running:
            for step in (1, 2, 4):
                total = total * jnp.where(row >= step, pltpu.roll(total, step, 0), 1.0)
            before.append(jnp.where(row >= 1, pltpu.roll(total, 1, 0), 1.0))
            after.append(jnp.broadcast_to(total[7:8], (8, GB)))
        return parts, before, after

    def plan(tile, state):
        count, spare = state
        live = loads[tile]
        for q in range(LBLK):
            work[count + q] = tile * LBLK + q
        return count + live, jnp.where(live < LBLK, tile * LBLK + LBLK - 1, spare)

    count, spare = lax.fori_loop(0, TILES, plan, (0, 0))
    for k in range(GROUP):
        work[count + k] = spare

    def leave(item):
        return pltpu.make_async_copy(out.at[item], out_hbm.at[item // LBLK, item % LBLK], sem)

    def group(step, carried):
        items = [work[step * GROUP + k] for k in range(GROUP)]
        done, values = [], []
        for item in items:
            tile, q = item // LBLK, item % LBLK
            alive = jnp.where(q < loads[tile], 1.0, 0.0)
            value = bins[lists[q, tile]]
            values.append(jnp.where(row == 3, value * alive, value))
        columns = jnp.concatenate(values, axis=0).T.astype(bf16)
        for k, item in enumerate(items):
            tile = item // LBLK
            pick = jnp.where(source == wanted + 8 * k, 1.0, 0.0).astype(bf16)
            wide = jnp.dot(columns, pick, preferred_element_type=f32)
            place_x = pixel_x + shift[0, tile]
            place_y = [pixel_y + shift[1, tile] + 8.0 * half for half in range(2)]
            done.append(one(wide, place_x, place_y))
        for item, (parts, before, after) in zip(items, done):
            fresh = item % LBLK == 0
            carried = [jnp.where(fresh, 1.0, value) for value in carried]
            for half in range(2):
                scale = carried[half] * before[half]
                rows = [part * scale for part in parts[half]]
                out[item, :, half * GB : half * GB + GB] = jnp.concatenate(rows, axis=0).astype(bf16)
            carried = [carried[half] * after[half] for half in range(2)]
        for k, item in enumerate(items):

            @pl.when(step * GROUP + k < count)
            def _():
                leave(item).start()

        return tuple(carried)

    lax.fori_loop(0, (count + GROUP - 1) // GROUP, group, (jnp.ones((8, GB), f32),) * 2)

    def arrived(i, unused):
        leave(0).wait()
        return unused

    lax.fori_loop(0, count, arrived, 0)


def weights(lists, loads, shift, screen, name):
    return pl.pallas_call(
        weights_kernel,
        out_shape=(jax.ShapeDtypeStruct((TILES, LBLK, GB, PIX), bf16), jax.ShapeDtypeStruct((8, GB), f32)),
        in_specs=[ANY] * 4,
        out_specs=(ANY, VM),
        scratch_shapes=[
            pltpu.SMEM((LBLK, TILES), jnp.int32),
            pltpu.SMEM((TILES,), jnp.int32),
            pltpu.SMEM((2, TILES), f32),
            pltpu.VMEM((N_TILE, BINS * 4, GB), bf16),
            pltpu.VMEM((N_TILE * BINS, 8, GB), f32),
            pltpu.VMEM((TILES * LBLK, GB, PIX), bf16),
            pltpu.SMEM((TILES * LBLK + LBLK,), jnp.int32),
            pltpu.SemaphoreType.DMA,
            pltpu.SemaphoreType.DMA((4,)),
        ],
        compiler_params=params(WEIGHTS_MIB),
        cost_estimate=pl.CostEstimate(
            flops=TILES * LBLK * GB * PIX * 14, bytes_accessed=10_000_000, transcendentals=TILES * LBLK * GB * PIX
        ),
        name=name,
    )(lists.T, loads, shift.T, screen)


def load_colors(blocks, colors, sems):
    return fetch([(block, colors.at[pl.ds(i * 32, 32)]) for i, block in enumerate(blocks)], sems)


def fetch_weights(loads, w_hbm, w, sems):
    def tile_start(tile, unused):
        for q in range(LBLK):

            @pl.when(q < loads[tile])
            def _():
                pltpu.make_async_copy(w_hbm.at[tile, q], w.at[tile, q], sems.at[tile]).start()

        return unused

    lax.fori_loop(0, TILES, tile_start, 0)


def over_tiles(loads, w_hbm, w, sems, body):
    def each_tile(tile, unused):
        live = loads[tile]
        for size in range(1, LBLK + 1):

            @pl.when(live == size)
            def _():
                pltpu.make_async_copy(
                    w_hbm.at[tile, pl.ds(0, size)], w.at[tile, pl.ds(0, size)], sems.at[tile]
                ).wait()
                body(tile, w[tile, :size].reshape(size * GB, PIX), size)

        return unused

    lax.fori_loop(0, TILES, each_tile, 0)


def picture(slots, tile, w, size, colors):
    row = jnp.concatenate([colors[slots[tile, q]] for q in range(size)], axis=1)
    return jnp.dot(row, w, preferred_element_type=f32)


def first_kernel(slots, loads, token, w_hbm, target_hbm, *rest):
    blocks, outs, (colors, w, target, total, sems, w_sems, t_sem) = rest[:8], rest[8:16], rest[16:]
    copies = load_colors(blocks, colors, sems) + fetch([(target_hbm, target)], t_sem)
    fetch_weights(loads, w_hbm, w, w_sems)

    def clear(i, unused):
        total[pl.ds(i * 8, 8)] = jnp.zeros((8, C, GB), f32)
        return unused

    lax.fori_loop(0, N_TILE, clear, 0)
    for copy in copies:
        copy.wait()

    def body(tile, w, size):
        residual = (picture(slots, tile, w, size, colors) - target[tile].astype(f32)).astype(bf16)
        pieces = lax.dot_general(residual, w, (((1,), (1,)), ((), ())), preferred_element_type=f32)
        for q in range(size):
            slot = slots[tile, q]
            total[slot] = total[slot] + pieces[:, q * GB : q * GB + GB]

    over_tiles(loads, w_hbm, w, w_sems, body)
    copies = fetch([(total.at[pl.ds(i * 32, 32)], out) for i, out in enumerate(outs)], sems)
    for copy in copies:
        copy.wait()


def first_render(slots, loads, token, w, target, blocks):
    return pl.pallas_call(
        first_kernel,
        out_shape=(jax.ShapeDtypeStruct((32, C, GB), f32),) * 8,
        in_specs=[SM, SM, ANY, ANY, ANY] + [ANY] * 8,
        out_specs=(ANY,) * 8,
        scratch_shapes=[
            pltpu.VMEM((N_TILE * BINS, C, GB), bf16),
            pltpu.VMEM((TILES, LBLK, GB, PIX), bf16),
            pltpu.VMEM((TILES, C, PIX), bf16),
            pltpu.VMEM((N_TILE * BINS, C, GB), f32),
            pltpu.SemaphoreType.DMA((8,)),
            pltpu.SemaphoreType.DMA((TILES,)),
            pltpu.SemaphoreType.DMA((1,)),
        ],
        compiler_params=params(RENDER_MIB),
        cost_estimate=pl.CostEstimate(flops=TILES * LBLK * C * GB * PIX * 4, bytes_accessed=25_000_000, transcendentals=0),
        name="first_render",
    )(slots, loads, token, w, target, *blocks)


def second_kernel(slots, loads, token, w_hbm, *rest):
    blocks, image, (colors, w, sems, w_sems) = rest[:8], rest[8], rest[9:]
    copies = load_colors(blocks, colors, sems)
    fetch_weights(loads, w_hbm, w, w_sems)
    for copy in copies:
        copy.wait()

    def body(tile, w, size):
        image[tile] = picture(slots, tile, w, size, colors)

    over_tiles(loads, w_hbm, w, w_sems, body)


def second_render(slots, loads, token, w, blocks):
    return pl.pallas_call(
        second_kernel,
        out_shape=jax.ShapeDtypeStruct((TILES, C, PIX), f32),
        in_specs=[SM, SM, ANY, ANY] + [ANY] * 8,
        out_specs=VM,
        scratch_shapes=[
            pltpu.VMEM((N_TILE * BINS, C, GB), bf16),
            pltpu.VMEM((TILES, LBLK, GB, PIX), bf16),
            pltpu.SemaphoreType.DMA((8,)),
            pltpu.SemaphoreType.DMA((TILES,)),
        ],
        compiler_params=params(RENDER_MIB),
        cost_estimate=pl.CostEstimate(flops=TILES * LBLK * C * GB * PIX * 2, bytes_accessed=14_000_000, transcendentals=0),
        name="second_render",
    )(slots, loads, token, w, *blocks)


def adam_kernel(owner, me, gradient, feat, m1, m2, colors, packed):
    g = reorder_wide(gradient[...].reshape(BINS * C, GB), True).reshape(BINS, C, GB)
    first_new = beta_first * m1[...] + (1.0 - beta_first) * g
    second_new = beta_second * m2[...] + (1.0 - beta_second) * g * g
    stepped = feat[...] - learn_rate * (first_new / bias_first) / (jnp.sqrt(second_new / bias_second) + adam_epsilon)
    flat = stepped.reshape(BINS * C, GB).astype(bf16)
    sent = reorder(flat, False).astype(bf16).reshape(BINS, C, GB)
    for s in range(BINS):
        w = owner[s]
        colors[w ^ me[0]] = sent[s]
        packed[w, 0:C] = stepped[s]
        packed[w, C : 2 * C] = first_new[s]
        packed[w, 2 * C : 3 * C] = second_new[s]


def adam(owner, me, gradient, feat, m1, m2):
    return pl.pallas_call(
        adam_kernel,
        out_shape=(
            jax.ShapeDtypeStruct((N_VIEW, C, GB), bf16),
            jax.ShapeDtypeStruct((N_VIEW, 3 * C, GB), f32),
        ),
        in_specs=[SM, SM, VM, VM, VM, VM],
        out_specs=(VM, VM),
        compiler_params=params(16),
        name="adam",
    )(owner, me, gradient, feat, m1, m2)


def device(x, y, c):
    return ((x % 4) * 4 + y % 4) * 2 + c


def shift_by(value, level, k):
    pairs = []
    for x in range(4):
        for y in range(4):
            for c in range(2):
                dx, dy = (k, 0) if c == level else (0, k)
                pairs.append((device(x, y, c), device(x + dx, y + dy, c)))
    return lax.ppermute(value, "tile", pairs)


def swap_core(value):
    pairs = [(t, t ^ 1) for t in range(N_TILE)]
    return lax.ppermute(value, "tile", pairs)


ORDER = (2, 1, 3)


def tie(*values):
    return lax.optimization_barrier(values)


def gather_line(colors):
    near = {0: colors}
    for k in ORDER:
        near[k] = shift_by(colors, 0, k)
    return jnp.concatenate([near[k] for k in range(4)], axis=0)


def gather_plane(line):
    plane = {0: line}
    for k in ORDER:
        plane[k] = shift_by(line, 1, k)
    return [plane[k] for k in range(4)]


def swapped(own):
    return list(own) + [swap_core(block) for block in own]


def scatter_far(parts):
    half16 = jnp.float16
    summed = {}
    for k in ORDER + (0,):
        summed[k] = parts[k] + swap_core(parts[4 + k])
    line = summed[0]
    for k in ORDER:
        line = line + shift_by(summed[k].astype(half16), 1, -k).astype(f32)
    return line


def scatter_near(line):
    half16 = jnp.float16
    total = line[0:BINS]
    for k in ORDER:
        total = total + shift_by(line[k * BINS : (k + 1) * BINS].astype(half16), 0, -k).astype(f32)
    return total


def color_slots(lists, within):
    me = lax.axis_index("tile")
    x, y, c = me // 8, (me // 2) % 4, me % 2
    owner = lists // BINS
    far_x = (x - owner // 8) % 4
    far_y = (y - (owner // 2) % 4) % 4
    core = owner % 2
    near = jnp.where(core == 0, far_x, far_y)
    far = jnp.where(core == 0, far_y, far_x)
    return (((core ^ c) * 4 + far) * 4 + near) * BINS + within


def exchange_views(colors):
    def step(value, r):
        return lax.ppermute(value, "view", [(v, v ^ r) for v in range(N_VIEW)])

    handed = step(colors[4:], 4)
    pairs = [jnp.concatenate([colors[r : r + 1], handed[r : r + 1]], axis=0) for r in range(4)]
    return jnp.concatenate([pairs[0]] + [step(pairs[r], r) for r in (1, 2, 3)], axis=0)


def place_of(view):
    r = view ^ lax.axis_index("view")
    return (r % 4) * 2 + r // 4


def across_view(value):
    return lax.all_to_all(value, "view", split_axis=0, concat_axis=0, tiled=True)


def across_tile(value):
    return lax.all_to_all(value, "tile", split_axis=0, concat_axis=0, tiled=True)


def local(
    features,
    moment_first,
    moment_second,
    positions,
    scales,
    opacity,
    cameras_first,
    shift_first,
    lists_first,
    loads_first,
    target,
    owner_after,
    cameras_second,
    shift_second,
    lists_second,
    loads_second,
):
    positions = jnp.transpose(positions, (1, 0, 2))
    colors, screen, geometry = prep(cameras_first, owner_after, features, positions, scales, opacity)
    screen = across_tile(screen)
    line, screen, geometry = tie(gather_line(colors), screen, geometry)
    geometry = across_view(geometry)
    own = gather_plane(line)
    w_first, token = weights(lists_first[0], loads_first[0], shift_first[0], screen, "weights_first")
    *own, token, geometry = tie(*own, token, geometry)
    slots = color_slots(lists_first[0], lists_first[0] % BINS)
    parts = first_render(slots, loads_first[0], token, w_first, target[0], swapped(own))
    screen = across_tile(screen_again(cameras_second[0], geometry))
    *parts, screen = tie(*parts, screen)
    w_second, token = weights(lists_second[0], loads_second[0], shift_second[0], screen, "weights_second")
    line, token = tie(scatter_far(parts), token)
    me = lax.axis_index("view").reshape(1)
    colors, packed = adam(owner_after, me, scatter_near(line), features, moment_first, moment_second)
    colors, packed = tie(exchange_views(colors), packed)
    packed = across_view(packed)
    blocks = swapped(gather_plane(gather_line(colors)))
    slots = color_slots(lists_second[0], place_of(lists_second[0] % BINS))
    image = second_render(slots, loads_second[0], token, w_second, blocks)
    new_features, new_first, new_second = (packed[:, i * C : i * C + C] for i in range(3))
    return (image[None], new_features, new_first, new_second)


def solution(mesh):
    return jax.shard_map(
        local,
        mesh=mesh,
        in_specs=(
            P(("view", "tile"), None, None),
            P(("view", "tile"), None, None),
            P(("view", "tile"), None, None),
            P(("view", "tile"), None, None),
            P(("view", "tile"), None),
            P(("view", "tile"), None),
            P("view", None, None),
            P("view", "tile", None),
            P("view", "tile", None),
            P("view", "tile"),
            P("view", "tile", None, None),
            P(("view", "tile")),
            P("view", None, None),
            P("view", "tile", None),
            P("view", "tile", None),
            P("view", "tile"),
        ),
        out_specs=(
            P("view", "tile", None, None),
            P(("view", "tile"), None, None),
            P(("view", "tile"), None, None),
            P(("view", "tile"), None, None),
        ),
        check_vma=False,
    )
```

```python
import functools

import jax
import jax.numpy as jnp
from jax import lax
from jax.experimental import pallas as pl
from jax.experimental.pallas import tpu as pltpu
from jax.sharding import PartitionSpec as P

C = 64
GB = 128
PIX = 256
SIDE = 16
LBLK = 8
TILES = 16
BINS = 8
N_VIEW = 8
N_TILE = 32
ROWS = GB // 8

beta_first = 0.9
beta_second = 0.999
learn_rate = 0.05
adam_epsilon = 1e-08
bias_first = 1.0 - 0.9**10
bias_second = 1.0 - 0.999**10

VM = pl.BlockSpec(memory_space=pltpu.VMEM)
SM = pl.BlockSpec(memory_space=pltpu.SMEM)
ANY = pl.BlockSpec(memory_space=pl.ANY)
GROUP = 8
WEIGHTS_MIB = 60
RENDER_MIB = 60
LOG2E = 1.4426950408889634
f32 = jnp.float32
bf16 = jnp.bfloat16


def params(mib, **more):
    return pltpu.CompilerParams(vmem_limit_bytes=mib * 1024 * 1024, **more)


def onehot(inverse):
    row = lax.broadcasted_iota(jnp.int32, (GB, GB), 0)
    col = lax.broadcasted_iota(jnp.int32, (GB, GB), 1)
    if inverse:
        row, col = col, row
    return jnp.where(col == (row % ROWS) * 8 + row // ROWS, 1.0, 0.0).astype(bf16)


def reorder(values, inverse):
    return jnp.dot(values, onehot(inverse), preferred_element_type=f32)


def reorder_wide(values, inverse):
    high = values.astype(bf16)
    rest = values - high.astype(f32)
    middle = rest.astype(bf16)
    low = (rest - middle.astype(f32)).astype(bf16)
    return (reorder(high, inverse) + reorder(middle, inverse)) + reorder(low, inverse)


def project_rows(p0, p1, p2, scales, opacity, camera):
    mean_x = camera[0, 0] * p0 + camera[0, 1] * p1 + camera[0, 2] * p2 + camera[0, 3]
    mean_y = camera[1, 0] * p0 + camera[1, 1] * p1 + camera[1, 2] * p2 + camera[1, 3]
    falloff = 0.5 / (scales * scales)
    opaque = 1.0 / (1.0 + jnp.exp(-opacity))
    stack = jnp.concatenate([mean_x, mean_y, falloff, opaque], axis=0)
    return reorder(stack.astype(bf16), False)


def screen_rows(stack):
    rows = [stack[k * BINS + b : k * BINS + b + 1] for b in range(BINS) for k in range(4)]
    return jnp.concatenate(rows, axis=0).astype(bf16)


def spread(stack, screen):
    rows = screen_rows(stack)
    for t in range(N_TILE):
        screen[t] = rows


def fetch(pairs, sems):
    copies = [pltpu.make_async_copy(source, to, sems.at[i]) for i, (source, to) in enumerate(pairs)]
    for copy in copies:
        copy.start()
    return copies


def prep_kernel(camera_hbm, owner_hbm, feat_hbm, pos_hbm, scales_hbm, opacity_hbm, colors, screen, geometry, *scratch):
    camera, owner, feat, pos, scales, opacity, sems = scratch
    copies = fetch(
        [
            (camera_hbm, camera),
            (owner_hbm, owner),
            (feat_hbm, feat),
            (pos_hbm, pos),
            (scales_hbm, scales),
            (opacity_hbm, opacity),
        ],
        sems,
    )
    for copy in copies:
        copy.wait()
    flat = feat[...].reshape(BINS * C, GB).astype(bf16)
    colors[...] = reorder(flat, False).astype(bf16).reshape(BINS, C, GB)
    stack = project_rows(pos[0], pos[1], pos[2], scales[...], opacity[...], camera.at[0])
    spread(stack, screen)
    for s in range(BINS):
        rows = [pos[k, s : s + 1] for k in range(3)]
        rows += [scales[s : s + 1], opacity[s : s + 1], jnp.zeros((3, GB), f32)]
        geometry[owner[s]] = jnp.concatenate(rows, axis=0)


def prep(camera, owner, feat, pos, scales, opacity):
    return pl.pallas_call(
        prep_kernel,
        out_shape=(
            jax.ShapeDtypeStruct((BINS, C, GB), bf16),
            jax.ShapeDtypeStruct((N_TILE, BINS * 4, GB), bf16),
            jax.ShapeDtypeStruct((N_VIEW, 8, GB), f32),
        ),
        in_specs=[ANY] * 6,
        out_specs=(VM, VM, VM),
        scratch_shapes=[
            pltpu.SMEM((1, 2, 4), f32),
            pltpu.SMEM((BINS,), jnp.int32),
            pltpu.VMEM((BINS, C, GB), f32),
            pltpu.VMEM((3, BINS, GB), f32),
            pltpu.VMEM((BINS, GB), f32),
            pltpu.VMEM((BINS, GB), f32),
            pltpu.SemaphoreType.DMA((6,)),
        ],
        compiler_params=params(60),
        name="prep",
    )(camera, owner, feat, pos, scales, opacity)


def screen_kernel(camera, geometry, screen):
    rows = [jnp.concatenate([geometry[b, k : k + 1] for b in range(BINS)], axis=0) for k in range(5)]
    spread(project_rows(*rows, camera), screen)


def screen_again(camera, geometry):
    return pl.pallas_call(
        screen_kernel,
        out_shape=jax.ShapeDtypeStruct((N_TILE, BINS * 4, GB), bf16),
        in_specs=[SM, VM],
        out_specs=VM,
        compiler_params=params(8),
        name="screen_again",
    )(camera, geometry)


def weights_kernel(lists_hbm, loads_hbm, shift_hbm, screen_hbm, out_hbm, token, *scratch):
    lists, loads, shift, screen, bins, out, work, sem, sems = scratch
    copies = fetch([(lists_hbm, lists), (loads_hbm, loads), (shift_hbm, shift), (screen_hbm, screen)], sems)
    token[...] = jnp.zeros((8, GB), f32)
    row = lax.broadcasted_iota(jnp.int32, (8, GB), 0)
    lane = lax.broadcasted_iota(jnp.int32, (8, GB), 1)
    pixel_x = (lane % SIDE).astype(f32) + 0.5
    pixel_y = (lane // SIDE).astype(f32) + 0.5
    for copy in copies:
        copy.wait()

    def widen(t, unused):
        rows = screen[t].astype(f32)
        for i in range(BINS // 2):
            two = rows[8 * i : 8 * i + 8]
            bins[t * BINS + 2 * i] = two
            bins[t * BINS + 2 * i + 1] = pltpu.roll(two, 4, 0)
        return unused

    lax.fori_loop(0, N_TILE, widen, 0, unroll=4)
    source = lax.broadcasted_iota(jnp.int32, (GROUP * 8, 4 * GB), 0)
    wanted = lax.broadcasted_iota(jnp.int32, (GROUP * 8, 4 * GB), 1) // GB

    def one(wide, place_x, place_y):
        running = [jnp.ones((8, GB), f32) for half in range(2)]
        parts = [[], []]
        for v in range(ROWS):
            some = wide[v * 8 : v * 8 + 8]
            mean_x, mean_y, fall, opaque = (some[:, k * GB : k * GB + GB] for k in range(4))
            fall = fall * -LOG2E
            delta_x = place_x - mean_x
            along_x = delta_x * delta_x * fall
            for half in range(2):
                delta_y = place_y[half] - mean_y
                part = opaque * jnp.exp2(along_x + delta_y * delta_y * fall) * running[half]
                parts[half].append(part)
                running[half] = running[half] - part
        before, after = [], []
        for total in running:
            for step in (1, 2, 4):
                total = total * jnp.where(row >= step, pltpu.roll(total, step, 0), 1.0)
            before.append(jnp.where(row >= 1, pltpu.roll(total, 1, 0), 1.0))
            after.append(jnp.broadcast_to(total[7:8], (8, GB)))
        return parts, before, after

    def plan(tile, state):
        count, spare = state
        live = loads[tile]
        for q in range(LBLK):
            work[count + q] = tile * LBLK + q
        return count + live, jnp.where(live < LBLK, tile * LBLK + LBLK - 1, spare)

    count, spare = lax.fori_loop(0, TILES, plan, (0, 0))
    for k in range(GROUP):
        work[count + k] = spare

    def leave(item):
        return pltpu.make_async_copy(out.at[item], out_hbm.at[item // LBLK, item % LBLK], sem)

    def group(step, carried):
        items = [work[step * GROUP + k] for k in range(GROUP)]
        done, values = [], []
        for item in items:
            tile, q = item // LBLK, item % LBLK
            alive = jnp.where(q < loads[tile], 1.0, 0.0)
            value = bins[lists[q, tile]]
            values.append(jnp.where(row == 3, value * alive, value))
        columns = jnp.concatenate(values, axis=0).T.astype(bf16)
        for k, item in enumerate(items):
            tile = item // LBLK
            pick = jnp.where(source == wanted + 8 * k, 1.0, 0.0).astype(bf16)
            wide = jnp.dot(columns, pick, preferred_element_type=f32)
            place_x = pixel_x + shift[0, tile]
            place_y = [pixel_y + shift[1, tile] + 8.0 * half for half in range(2)]
            done.append(one(wide, place_x, place_y))
        for item, (parts, before, after) in zip(items, done):
            fresh = item % LBLK == 0
            carried = [jnp.where(fresh, 1.0, value) for value in carried]
            for half in range(2):
                scale = carried[half] * before[half]
                rows = [part * scale for part in parts[half]]
                out[item, :, half * GB : half * GB + GB] = jnp.concatenate(rows, axis=0).astype(bf16)
            carried = [carried[half] * after[half] for half in range(2)]
        for k, item in enumerate(items):

            @pl.when(step * GROUP + k < count)
            def _():
                leave(item).start()

        return tuple(carried)

    lax.fori_loop(0, (count + GROUP - 1) // GROUP, group, (jnp.ones((8, GB), f32),) * 2)

    def arrived(i, unused):
        leave(0).wait()
        return unused

    lax.fori_loop(0, count, arrived, 0)


def weights(lists, loads, shift, screen, name):
    return pl.pallas_call(
        weights_kernel,
        out_shape=(jax.ShapeDtypeStruct((TILES, LBLK, GB, PIX), bf16), jax.ShapeDtypeStruct((8, GB), f32)),
        in_specs=[ANY] * 4,
        out_specs=(ANY, VM),
        scratch_shapes=[
            pltpu.SMEM((LBLK, TILES), jnp.int32),
            pltpu.SMEM((TILES,), jnp.int32),
            pltpu.SMEM((2, TILES), f32),
            pltpu.VMEM((N_TILE, BINS * 4, GB), bf16),
            pltpu.VMEM((N_TILE * BINS, 8, GB), f32),
            pltpu.VMEM((TILES * LBLK, GB, PIX), bf16),
            pltpu.SMEM((TILES * LBLK + LBLK,), jnp.int32),
            pltpu.SemaphoreType.DMA,
            pltpu.SemaphoreType.DMA((4,)),
        ],
        compiler_params=params(WEIGHTS_MIB),
        cost_estimate=pl.CostEstimate(
            flops=TILES * LBLK * GB * PIX * 14, bytes_accessed=10_000_000, transcendentals=TILES * LBLK * GB * PIX
        ),
        name=name,
    )(lists.T, loads, shift.T, screen)


def load_colors(blocks, colors, sems):
    return fetch([(block, colors.at[pl.ds(i * 32, 32)]) for i, block in enumerate(blocks)], sems)


def fetch_weights(loads, w_hbm, w, sems):
    def tile_start(tile, unused):
        for q in range(LBLK):

            @pl.when(q < loads[tile])
            def _():
                pltpu.make_async_copy(w_hbm.at[tile, q], w.at[tile, q], sems.at[tile]).start()

        return unused

    lax.fori_loop(0, TILES, tile_start, 0)


def over_tiles(loads, w_hbm, w, sems, body):
    def each_tile(tile, unused):
        live = loads[tile]
        for size in range(1, LBLK + 1):

            @pl.when(live == size)
            def _():
                pltpu.make_async_copy(
                    w_hbm.at[tile, pl.ds(0, size)], w.at[tile, pl.ds(0, size)], sems.at[tile]
                ).wait()
                body(tile, w[tile, :size].reshape(size * GB, PIX), size)

        return unused

    lax.fori_loop(0, TILES, each_tile, 0)


def picture(slots, tile, w, size, colors):
    row = jnp.concatenate([colors[slots[tile, q]] for q in range(size)], axis=1)
    return jnp.dot(row, w, preferred_element_type=f32)


def first_kernel(slots, loads, token, w_hbm, target_hbm, *rest):
    blocks, outs, (colors, w, target, total, sems, w_sems, t_sem) = rest[:8], rest[8:16], rest[16:]
    copies = load_colors(blocks, colors, sems) + fetch([(target_hbm, target)], t_sem)
    fetch_weights(loads, w_hbm, w, w_sems)

    def clear(i, unused):
        total[pl.ds(i * 8, 8)] = jnp.zeros((8, C, GB), f32)
        return unused

    lax.fori_loop(0, N_TILE, clear, 0)
    for copy in copies:
        copy.wait()

    def body(tile, w, size):
        residual = (picture(slots, tile, w, size, colors) - target[tile].astype(f32)).astype(bf16)
        pieces = lax.dot_general(residual, w, (((1,), (1,)), ((), ())), preferred_element_type=f32)
        for q in range(size):
            slot = slots[tile, q]
            total[slot] = total[slot] + pieces[:, q * GB : q * GB + GB]

    over_tiles(loads, w_hbm, w, w_sems, body)
    copies = fetch([(total.at[pl.ds(i * 32, 32)], out) for i, out in enumerate(outs)], sems)
    for copy in copies:
        copy.wait()


def first_render(slots, loads, token, w, target, blocks):
    return pl.pallas_call(
        first_kernel,
        out_shape=(jax.ShapeDtypeStruct((32, C, GB), f32),) * 8,
        in_specs=[SM, SM, ANY, ANY, ANY] + [ANY] * 8,
        out_specs=(ANY,) * 8,
        scratch_shapes=[
            pltpu.VMEM((N_TILE * BINS, C, GB), bf16),
            pltpu.VMEM((TILES, LBLK, GB, PIX), bf16),
            pltpu.VMEM((TILES, C, PIX), bf16),
            pltpu.VMEM((N_TILE * BINS, C, GB), f32),
            pltpu.SemaphoreType.DMA((8,)),
            pltpu.SemaphoreType.DMA((TILES,)),
            pltpu.SemaphoreType.DMA((1,)),
        ],
        compiler_params=params(RENDER_MIB),
        cost_estimate=pl.CostEstimate(flops=TILES * LBLK * C * GB * PIX * 4, bytes_accessed=25_000_000, transcendentals=0),
        name="first_render",
    )(slots, loads, token, w, target, *blocks)


def second_kernel(slots, loads, token, w_hbm, *rest):
    blocks, image, (colors, w, sems, w_sems) = rest[:8], rest[8], rest[9:]
    copies = load_colors(blocks, colors, sems)
    fetch_weights(loads, w_hbm, w, w_sems)
    for copy in copies:
        copy.wait()

    def body(tile, w, size):
        image[tile] = picture(slots, tile, w, size, colors)

    over_tiles(loads, w_hbm, w, w_sems, body)


def second_render(slots, loads, token, w, blocks):
    return pl.pallas_call(
        second_kernel,
        out_shape=jax.ShapeDtypeStruct((TILES, C, PIX), f32),
        in_specs=[SM, SM, ANY, ANY] + [ANY] * 8,
        out_specs=VM,
        scratch_shapes=[
            pltpu.VMEM((N_TILE * BINS, C, GB), bf16),
            pltpu.VMEM((TILES, LBLK, GB, PIX), bf16),
            pltpu.SemaphoreType.DMA((8,)),
            pltpu.SemaphoreType.DMA((TILES,)),
        ],
        compiler_params=params(RENDER_MIB),
        cost_estimate=pl.CostEstimate(flops=TILES * LBLK * C * GB * PIX * 2, bytes_accessed=14_000_000, transcendentals=0),
        name="second_render",
    )(slots, loads, token, w, *blocks)


def adam_kernel(owner, me, gradient, feat, m1, m2, colors, packed):
    g = reorder_wide(gradient[...].reshape(BINS * C, GB), True).reshape(BINS, C, GB)
    first_new = beta_first * m1[...] + (1.0 - beta_first) * g
    second_new = beta_second * m2[...] + (1.0 - beta_second) * g * g
    stepped = feat[...] - learn_rate * (first_new / bias_first) / (jnp.sqrt(second_new / bias_second) + adam_epsilon)
    flat = stepped.reshape(BINS * C, GB).astype(bf16)
    sent = reorder(flat, False).astype(bf16).reshape(BINS, C, GB)
    for s in range(BINS):
        w = owner[s]
        colors[w ^ me[0]] = sent[s]
        packed[w, 0:C] = stepped[s]
        packed[w, C : 2 * C] = first_new[s]
        packed[w, 2 * C : 3 * C] = second_new[s]


def adam(owner, me, gradient, feat, m1, m2):
    return pl.pallas_call(
        adam_kernel,
        out_shape=(
            jax.ShapeDtypeStruct((N_VIEW, C, GB), bf16),
            jax.ShapeDtypeStruct((N_VIEW, 3 * C, GB), f32),
        ),
        in_specs=[SM, SM, VM, VM, VM, VM],
        out_specs=(VM, VM),
        compiler_params=params(16),
        name="adam",
    )(owner, me, gradient, feat, m1, m2)


def device(x, y, c):
    return ((x % 4) * 4 + y % 4) * 2 + c


def shift_by(value, level, k):
    pairs = []
    for x in range(4):
        for y in range(4):
            for c in range(2):
                dx, dy = (k, 0) if c == level else (0, k)
                pairs.append((device(x, y, c), device(x + dx, y + dy, c)))
    return lax.ppermute(value, "tile", pairs)


def swap_core(value):
    pairs = [(t, t ^ 1) for t in range(N_TILE)]
    return lax.ppermute(value, "tile", pairs)


ORDER = (2, 1, 3)


def tie(*values):
    return lax.optimization_barrier(values)


def gather_line(colors):
    near = {0: colors}
    for k in ORDER:
        near[k] = shift_by(colors, 0, k)
    return jnp.concatenate([near[k] for k in range(4)], axis=0)


def gather_plane(line, later=None):
    plane = {0: line}
    for k in ORDER:
        if later is not None and k == ORDER[-1]:
            line, later = tie(line, later)
        plane[k] = shift_by(line, 1, k)
    own = [plane[k] for k in range(4)]
    return own if later is None else (own, later)


def swapped(own):
    return list(own) + [swap_core(block) for block in own]


def scatter_far(parts, later):
    half16 = jnp.float16
    sent = {}
    for k in ORDER:
        sent[k] = (parts[k] + swap_core(parts[4 + k])).astype(half16)
    line = parts[0] + swap_core(parts[4])
    sent[3], later = tie(sent[3], later)
    for k in ORDER:
        line = line + shift_by(sent[k], 1, -k).astype(f32)
    return line, later


def scatter_near(line):
    half16 = jnp.float16
    total = line[0:BINS]
    for k in ORDER:
        total = total + shift_by(line[k * BINS : (k + 1) * BINS].astype(half16), 0, -k).astype(f32)
    return total


def color_slots(lists, within):
    me = lax.axis_index("tile")
    x, y, c = me // 8, (me // 2) % 4, me % 2
    owner = lists // BINS
    far_x = (x - owner // 8) % 4
    far_y = (y - (owner // 2) % 4) % 4
    core = owner % 2
    near = jnp.where(core == 0, far_x, far_y)
    far = jnp.where(core == 0, far_y, far_x)
    return (((core ^ c) * 4 + far) * 4 + near) * BINS + within


def exchange_views(colors):
    def step(r):
        return lax.ppermute(colors[r : r + 1], "view", [(v, v ^ r) for v in range(N_VIEW)])

    got = {r: step(r) for r in (4, 5, 3, 6, 2, 7, 1)}
    return jnp.concatenate([colors[0:1]] + [got[r] for r in range(1, N_VIEW)], axis=0)


def place_of(view):
    return view ^ lax.axis_index("view")


def across_view(value):
    return lax.all_to_all(value, "view", split_axis=0, concat_axis=0, tiled=True)


def across_tile(value):
    return lax.all_to_all(value, "tile", split_axis=0, concat_axis=0, tiled=True)


def local(
    features,
    moment_first,
    moment_second,
    positions,
    scales,
    opacity,
    cameras_first,
    shift_first,
    lists_first,
    loads_first,
    target,
    owner_after,
    cameras_second,
    shift_second,
    lists_second,
    loads_second,
):
    positions = jnp.transpose(positions, (1, 0, 2))
    colors, screen, geometry = prep(cameras_first, owner_after, features, positions, scales, opacity)
    screen = across_tile(screen)
    own, screen = gather_plane(gather_line(colors), screen)
    w_first, token = weights(lists_first[0], loads_first[0], shift_first[0], screen, "weights_first")
    *own, token = tie(*own, token)
    slots = color_slots(lists_first[0], lists_first[0] % BINS)
    parts = first_render(slots, loads_first[0], token, w_first, target[0], swapped(own))
    line, geometry = scatter_far(parts, geometry)
    screen = screen_again(cameras_second[0], across_view(geometry))
    line, screen = tie(line, screen)
    gradient, screen = tie(scatter_near(line), across_tile(screen))
    w_second, token = weights(lists_second[0], loads_second[0], shift_second[0], screen, "weights_second")
    me = lax.axis_index("view").reshape(1)
    colors, packed = adam(owner_after, me, gradient, features, moment_first, moment_second)
    colors, packed = tie(exchange_views(colors), packed)
    packed = across_view(packed)
    *own, token = tie(*gather_plane(gather_line(colors)), token)
    blocks = swapped(own)
    slots = color_slots(lists_second[0], place_of(lists_second[0] % BINS))
    image = second_render(slots, loads_second[0], token, w_second, blocks)
    new_features, new_first, new_second = (packed[:, i * C : i * C + C] for i in range(3))
    return (image[None], new_features, new_first, new_second)


def solution(mesh):
    return jax.shard_map(
        local,
        mesh=mesh,
        in_specs=(
            P(("view", "tile"), None, None),
            P(("view", "tile"), None, None),
            P(("view", "tile"), None, None),
            P(("view", "tile"), None, None),
            P(("view", "tile"), None),
            P(("view", "tile"), None),
            P("view", None, None),
            P("view", "tile", None),
            P("view", "tile", None),
            P("view", "tile"),
            P("view", "tile", None, None),
            P(("view", "tile")),
            P("view", None, None),
            P("view", "tile", None),
            P("view", "tile", None),
            P("view", "tile"),
        ),
        out_specs=(
            P("view", "tile", None, None),
            P(("view", "tile"), None, None),
            P(("view", "tile"), None, None),
            P(("view", "tile"), None, None),
        ),
        check_vma=False,
    )
```

```python
import functools

import jax
import jax.numpy as jnp
from jax import lax
from jax.experimental import pallas as pl
from jax.experimental.pallas import tpu as pltpu
from jax.sharding import PartitionSpec as P

C = 64
GB = 128
PIX = 256
SIDE = 16
LBLK = 8
TILES = 16
BINS = 8
N_VIEW = 8
N_TILE = 32
ROWS = GB // 8

beta_first = 0.9
beta_second = 0.999
learn_rate = 0.05
adam_epsilon = 1e-08
bias_first = 1.0 - 0.9**10
bias_second = 1.0 - 0.999**10

VM = pl.BlockSpec(memory_space=pltpu.VMEM)
SM = pl.BlockSpec(memory_space=pltpu.SMEM)
ANY = pl.BlockSpec(memory_space=pl.ANY)
GROUP = 8
WEIGHTS_MIB = 60
RENDER_MIB = 34
SECOND_MIB = 48
LOG2E = 1.4426950408889634
f32 = jnp.float32
bf16 = jnp.bfloat16


def params(mib, **more):
    return pltpu.CompilerParams(vmem_limit_bytes=mib * 1024 * 1024, **more)


def onehot(inverse):
    row = lax.broadcasted_iota(jnp.int32, (GB, GB), 0)
    col = lax.broadcasted_iota(jnp.int32, (GB, GB), 1)
    if inverse:
        row, col = col, row
    return jnp.where(col == (row % ROWS) * 8 + row // ROWS, 1.0, 0.0).astype(bf16)


def reorder(values, inverse):
    return jnp.dot(values, onehot(inverse), preferred_element_type=f32)


def reorder_wide(values, inverse):
    high = values.astype(bf16)
    rest = values - high.astype(f32)
    middle = rest.astype(bf16)
    low = (rest - middle.astype(f32)).astype(bf16)
    return (reorder(high, inverse) + reorder(middle, inverse)) + reorder(low, inverse)


def project_rows(p0, p1, p2, scales, opacity, camera):
    mean_x = camera[0, 0] * p0 + camera[0, 1] * p1 + camera[0, 2] * p2 + camera[0, 3]
    mean_y = camera[1, 0] * p0 + camera[1, 1] * p1 + camera[1, 2] * p2 + camera[1, 3]
    falloff = 0.5 / (scales * scales)
    opaque = 1.0 / (1.0 + jnp.exp(-opacity))
    stack = jnp.concatenate([mean_x, mean_y, falloff, opaque], axis=0)
    return reorder(stack.astype(bf16), False)


def screen_rows(stack):
    rows = [stack[k * BINS + b : k * BINS + b + 1] for b in range(BINS) for k in range(4)]
    return jnp.concatenate(rows, axis=0).astype(bf16)


def spread(stack, screen):
    rows = screen_rows(stack)
    for t in range(N_TILE):
        screen[t] = rows


def fetch(pairs, sems):
    copies = [pltpu.make_async_copy(source, to, sems.at[i]) for i, (source, to) in enumerate(pairs)]
    for copy in copies:
        copy.start()
    return copies


def prep_kernel(camera_hbm, owner_hbm, feat_hbm, pos_hbm, scales_hbm, opacity_hbm, colors, screen, geometry, *scratch):
    camera, owner, feat, pos, scales, opacity, sems = scratch
    copies = fetch(
        [
            (camera_hbm, camera),
            (owner_hbm, owner),
            (feat_hbm, feat),
            (pos_hbm, pos),
            (scales_hbm, scales),
            (opacity_hbm, opacity),
        ],
        sems,
    )
    for copy in copies:
        copy.wait()
    flat = feat[...].reshape(BINS * C, GB).astype(bf16)
    colors[...] = reorder(flat, False).astype(bf16).reshape(BINS, C, GB)
    stack = project_rows(pos[0], pos[1], pos[2], scales[...], opacity[...], camera.at[0])
    spread(stack, screen)
    for s in range(BINS):
        rows = [pos[k, s : s + 1] for k in range(3)]
        rows += [scales[s : s + 1], opacity[s : s + 1], jnp.zeros((3, GB), f32)]
        geometry[owner[s]] = jnp.concatenate(rows, axis=0)


def prep(camera, owner, feat, pos, scales, opacity):
    return pl.pallas_call(
        prep_kernel,
        out_shape=(
            jax.ShapeDtypeStruct((BINS, C, GB), bf16),
            jax.ShapeDtypeStruct((N_TILE, BINS * 4, GB), bf16),
            jax.ShapeDtypeStruct((N_VIEW, 8, GB), f32),
        ),
        in_specs=[ANY] * 6,
        out_specs=(VM, VM, VM),
        scratch_shapes=[
            pltpu.SMEM((1, 2, 4), f32),
            pltpu.SMEM((BINS,), jnp.int32),
            pltpu.VMEM((BINS, C, GB), f32),
            pltpu.VMEM((3, BINS, GB), f32),
            pltpu.VMEM((BINS, GB), f32),
            pltpu.VMEM((BINS, GB), f32),
            pltpu.SemaphoreType.DMA((6,)),
        ],
        compiler_params=params(60),
        name="prep",
    )(camera, owner, feat, pos, scales, opacity)


def screen_kernel(camera, geometry, screen):
    rows = [jnp.concatenate([geometry[b, k : k + 1] for b in range(BINS)], axis=0) for k in range(5)]
    spread(project_rows(*rows, camera), screen)


def screen_again(camera, geometry):
    return pl.pallas_call(
        screen_kernel,
        out_shape=jax.ShapeDtypeStruct((N_TILE, BINS * 4, GB), bf16),
        in_specs=[SM, VM],
        out_specs=VM,
        compiler_params=params(8),
        name="screen_again",
    )(camera, geometry)


def weights_kernel(lists_hbm, loads_hbm, shift_hbm, screen_hbm, out_hbm, token, *scratch):
    lists, loads, shift, screen, bins, out, work, sem, sems = scratch
    copies = fetch([(lists_hbm, lists), (loads_hbm, loads), (shift_hbm, shift), (screen_hbm, screen)], sems)
    token[...] = jnp.zeros((8, GB), jnp.int32)
    row = lax.broadcasted_iota(jnp.int32, (8, GB), 0)
    lane = lax.broadcasted_iota(jnp.int32, (8, GB), 1)
    pixel_x = (lane % SIDE).astype(f32) + 0.5
    pixel_y = (lane // SIDE).astype(f32) + 0.5
    for copy in copies:
        copy.wait()

    def widen(t, unused):
        rows = screen[t].astype(f32)
        for i in range(BINS // 2):
            two = rows[8 * i : 8 * i + 8]
            bins[t * BINS + 2 * i] = two
            bins[t * BINS + 2 * i + 1] = pltpu.roll(two, 4, 0)
        return unused

    lax.fori_loop(0, N_TILE, widen, 0, unroll=4)
    source = lax.broadcasted_iota(jnp.int32, (GROUP * 8, 4 * GB), 0)
    wanted = lax.broadcasted_iota(jnp.int32, (GROUP * 8, 4 * GB), 1) // GB

    def one(wide, place_x, place_y):
        running = [jnp.ones((8, GB), f32) for half in range(2)]
        parts = [[], []]
        for v in range(ROWS):
            some = wide[v * 8 : v * 8 + 8]
            mean_x, mean_y, fall, opaque = (some[:, k * GB : k * GB + GB] for k in range(4))
            fall = fall * -LOG2E
            delta_x = place_x - mean_x
            along_x = delta_x * delta_x * fall
            for half in range(2):
                delta_y = place_y[half] - mean_y
                part = opaque * jnp.exp2(along_x + delta_y * delta_y * fall) * running[half]
                parts[half].append(part)
                running[half] = running[half] - part
        before, after = [], []
        for total in running:
            for step in (1, 2, 4):
                total = total * jnp.where(row >= step, pltpu.roll(total, step, 0), 1.0)
            before.append(jnp.where(row >= 1, pltpu.roll(total, 1, 0), 1.0))
            after.append(jnp.broadcast_to(total[7:8], (8, GB)))
        return parts, before, after

    def plan(tile, state):
        count, spare = state
        live = loads[tile]
        for q in range(LBLK):
            work[count + q] = tile * LBLK + q
        return count + live, jnp.where(live < LBLK, tile * LBLK + LBLK - 1, spare)

    count, spare = lax.fori_loop(0, TILES, plan, (0, 0))
    for k in range(GROUP):
        work[count + k] = spare

    def leave(item):
        return pltpu.make_async_copy(out.at[item], out_hbm.at[item // LBLK, item % LBLK], sem)

    def group(step, carried):
        items = [work[step * GROUP + k] for k in range(GROUP)]
        done, values = [], []
        for item in items:
            tile, q = item // LBLK, item % LBLK
            alive = jnp.where(q < loads[tile], 1.0, 0.0)
            value = bins[lists[q, tile]]
            values.append(jnp.where(row == 3, value * alive, value))
        columns = jnp.concatenate(values, axis=0).T.astype(bf16)
        for k, item in enumerate(items):
            tile = item // LBLK
            pick = jnp.where(source == wanted + 8 * k, 1.0, 0.0).astype(bf16)
            wide = jnp.dot(columns, pick, preferred_element_type=f32)
            place_x = pixel_x + shift[0, tile]
            place_y = [pixel_y + shift[1, tile] + 8.0 * half for half in range(2)]
            done.append(one(wide, place_x, place_y))
        for item, (parts, before, after) in zip(items, done):
            fresh = item % LBLK == 0
            carried = [jnp.where(fresh, 1.0, value) for value in carried]
            for half in range(2):
                scale = carried[half] * before[half]
                rows = [part * scale for part in parts[half]]
                out[item, :, half * GB : half * GB + GB] = jnp.concatenate(rows, axis=0).astype(bf16)
            carried = [carried[half] * after[half] for half in range(2)]
        for k, item in enumerate(items):

            @pl.when(step * GROUP + k < count)
            def _():
                leave(item).start()

        return tuple(carried)

    lax.fori_loop(0, (count + GROUP - 1) // GROUP, group, (jnp.ones((8, GB), f32),) * 2)

    def arrived(i, unused):
        leave(0).wait()
        return unused

    lax.fori_loop(0, count, arrived, 0)


def weights(lists, loads, shift, screen, name):
    return pl.pallas_call(
        weights_kernel,
        out_shape=(jax.ShapeDtypeStruct((TILES, LBLK, GB, PIX), bf16), jax.ShapeDtypeStruct((8, GB), jnp.int32)),
        in_specs=[ANY] * 4,
        out_specs=(ANY, VM),
        scratch_shapes=[
            pltpu.SMEM((LBLK, TILES), jnp.int32),
            pltpu.SMEM((TILES,), jnp.int32),
            pltpu.SMEM((2, TILES), f32),
            pltpu.VMEM((N_TILE, BINS * 4, GB), bf16),
            pltpu.VMEM((N_TILE * BINS, 8, GB), f32),
            pltpu.VMEM((TILES * LBLK, GB, PIX), bf16),
            pltpu.SMEM((TILES * LBLK + LBLK,), jnp.int32),
            pltpu.SemaphoreType.DMA,
            pltpu.SemaphoreType.DMA((4,)),
        ],
        compiler_params=params(WEIGHTS_MIB),
        cost_estimate=pl.CostEstimate(
            flops=TILES * LBLK * GB * PIX * 14, bytes_accessed=10_000_000, transcendentals=TILES * LBLK * GB * PIX
        ),
        name=name,
    )(lists.T, loads, shift.T, screen)


def load_colors(blocks, colors, sems):
    return fetch([(block, colors.at[pl.ds(i * 32, 32)]) for i, block in enumerate(blocks)], sems)


def fetch_weights(loads, w_hbm, w, sems):
    def tile_start(tile, unused):
        for q in range(LBLK):

            @pl.when(q < loads[tile])
            def _():
                pltpu.make_async_copy(w_hbm.at[tile, q], w.at[tile, q], sems.at[tile]).start()

        return unused

    lax.fori_loop(0, TILES, tile_start, 0)


def over_tiles(loads, w_hbm, w, sems, body):
    def each_tile(tile, unused):
        live = loads[tile]
        for size in range(1, LBLK + 1):

            @pl.when(live == size)
            def _():
                pltpu.make_async_copy(
                    w_hbm.at[tile, pl.ds(0, size)], w.at[tile, pl.ds(0, size)], sems.at[tile]
                ).wait()
                body(tile, w[tile, :size].reshape(size * GB, PIX), size)

        return unused

    lax.fori_loop(0, TILES, each_tile, 0)


def picture(slots, tile, w, size, colors):
    row = jnp.concatenate([colors[slots[tile, q]] for q in range(size)], axis=1)
    return jnp.dot(row, w, preferred_element_type=f32)


def first_kernel(slots, loads, w_hbm, target_hbm, *rest):
    blocks, outs, (colors, w, target, total, sems, w_sems, t_sem) = rest[:8], rest[8:16], rest[16:]
    copies = load_colors(blocks, colors, sems) + fetch([(target_hbm, target)], t_sem)
    fetch_weights(loads, w_hbm, w, w_sems)

    def clear(i, unused):
        total[pl.ds(i * 8, 8)] = jnp.zeros((8, C, GB), f32)
        return unused

    lax.fori_loop(0, N_TILE, clear, 0)
    for copy in copies:
        copy.wait()

    def body(tile, w, size):
        residual = (picture(slots, tile, w, size, colors) - target[tile].astype(f32)).astype(bf16)
        pieces = lax.dot_general(residual, w, (((1,), (1,)), ((), ())), preferred_element_type=f32)
        for q in range(size):
            slot = slots[tile, q]
            total[slot] = total[slot] + pieces[:, q * GB : q * GB + GB]

    over_tiles(loads, w_hbm, w, w_sems, body)
    copies = fetch([(total.at[pl.ds(i * 32, 32)], out) for i, out in enumerate(outs)], sems)
    for copy in copies:
        copy.wait()


def first_render(slots, loads, w, target, blocks):
    return pl.pallas_call(
        first_kernel,
        out_shape=(jax.ShapeDtypeStruct((32, C, GB), f32),) * 8,
        in_specs=[SM, SM, ANY, ANY] + [ANY] * 8,
        out_specs=(ANY,) * 8,
        scratch_shapes=[
            pltpu.VMEM((N_TILE * BINS, C, GB), bf16),
            pltpu.VMEM((TILES, LBLK, GB, PIX), bf16),
            pltpu.VMEM((TILES, C, PIX), bf16),
            pltpu.VMEM((N_TILE * BINS, C, GB), f32),
            pltpu.SemaphoreType.DMA((8,)),
            pltpu.SemaphoreType.DMA((TILES,)),
            pltpu.SemaphoreType.DMA((1,)),
        ],
        compiler_params=params(RENDER_MIB),
        cost_estimate=pl.CostEstimate(flops=TILES * LBLK * C * GB * PIX * 4, bytes_accessed=25_000_000, transcendentals=0),
        name="first_render",
    )(slots, loads, w, target, *blocks)


def second_kernel(slots, loads, w_hbm, *rest):
    blocks, image, (colors, w, sems, w_sems) = rest[:8], rest[8], rest[9:]
    copies = load_colors(blocks, colors, sems)
    fetch_weights(loads, w_hbm, w, w_sems)
    for copy in copies:
        copy.wait()

    def body(tile, w, size):
        image[tile] = picture(slots, tile, w, size, colors)

    over_tiles(loads, w_hbm, w, w_sems, body)


def second_render(slots, loads, w, blocks):
    return pl.pallas_call(
        second_kernel,
        out_shape=jax.ShapeDtypeStruct((TILES, C, PIX), f32),
        in_specs=[SM, SM, ANY] + [ANY] * 8,
        out_specs=VM,
        scratch_shapes=[
            pltpu.VMEM((N_TILE * BINS, C, GB), bf16),
            pltpu.VMEM((TILES, LBLK, GB, PIX), bf16),
            pltpu.SemaphoreType.DMA((8,)),
            pltpu.SemaphoreType.DMA((TILES,)),
        ],
        compiler_params=params(SECOND_MIB),
        cost_estimate=pl.CostEstimate(flops=TILES * LBLK * C * GB * PIX * 2, bytes_accessed=14_000_000, transcendentals=0),
        name="second_render",
    )(slots, loads, w, *blocks)


def adam_kernel(owner, me, gradient, feat, m1, m2, close, away, packed, colors):
    g = reorder_wide(gradient[...].reshape(BINS * C, GB), True).reshape(BINS, C, GB)
    first_new = beta_first * m1[...] + (1.0 - beta_first) * g
    second_new = beta_second * m2[...] + (1.0 - beta_second) * g * g
    stepped = feat[...] - learn_rate * (first_new / bias_first) / (jnp.sqrt(second_new / bias_second) + adam_epsilon)
    flat = stepped.reshape(BINS * C, GB).astype(bf16)
    sent = reorder(flat, False).astype(bf16).reshape(BINS, C, GB)
    for s in range(BINS):
        w = owner[s]
        colors[w ^ me[0]] = sent[s]
        packed[w, 0:C] = stepped[s]
        packed[w, C : 2 * C] = first_new[s]
        packed[w, 2 * C : 3 * C] = second_new[s]
    close[...] = colors[0:4]
    away[...] = colors[4:]


def adam(owner, me, gradient, feat, m1, m2):
    return pl.pallas_call(
        adam_kernel,
        out_shape=(
            jax.ShapeDtypeStruct((N_VIEW // 2, C, GB), bf16),
            jax.ShapeDtypeStruct((N_VIEW // 2, C, GB), bf16),
            jax.ShapeDtypeStruct((N_VIEW, 3 * C, GB), f32),
        ),
        in_specs=[SM, SM, VM, VM, VM, VM],
        out_specs=(VM, VM, VM),
        scratch_shapes=[pltpu.VMEM((N_VIEW, C, GB), bf16)],
        compiler_params=params(16),
        name="adam",
    )(owner, me, gradient, feat, m1, m2)


def device(x, y, c):
    return ((x % 4) * 4 + y % 4) * 2 + c


def shift_by(value, level, k):
    pairs = []
    for x in range(4):
        for y in range(4):
            for c in range(2):
                dx, dy = (k, 0) if c == level else (0, k)
                pairs.append((device(x, y, c), device(x + dx, y + dy, c)))
    return lax.ppermute(value, "tile", pairs)


def swap_core(value):
    pairs = [(t, t ^ 1) for t in range(N_TILE)]
    return lax.ppermute(value, "tile", pairs)


ORDER = (2, 1, 3)


def tie(*values):
    return lax.optimization_barrier(values)


def gather_line(colors):
    near = {0: colors}
    for k in ORDER:
        near[k] = shift_by(colors, 0, k)
    return jnp.concatenate([near[k] for k in range(4)], axis=0)


def gather_plane(line, later=None):
    plane = {0: line}
    for k in ORDER:
        if later is not None and k == ORDER[-1]:
            line, later = tie(line, later)
        plane[k] = shift_by(line, 1, k)
    own = [plane[k] for k in range(4)]
    return own if later is None else (own, later)


def swapped(own):
    return list(own) + [swap_core(block) for block in own]


def scatter_far(parts, later):
    half16 = jnp.float16
    sent = {}
    for k in ORDER:
        sent[k] = (parts[k] + swap_core(parts[4 + k])).astype(half16)
    line = parts[0] + swap_core(parts[4])
    sent[3], later = tie(sent[3], later)
    for k in ORDER:
        line = line + shift_by(sent[k], 1, -k).astype(f32)
    return line, later


def scatter_near(line):
    half16 = jnp.float16
    total = line[0:BINS]
    for k in ORDER:
        total = total + shift_by(line[k * BINS : (k + 1) * BINS].astype(half16), 0, -k).astype(f32)
    return total


def color_slots(lists, within):
    me = lax.axis_index("tile")
    x, y, c = me // 8, (me // 2) % 4, me % 2
    owner = lists // BINS
    far_x = (x - owner // 8) % 4
    far_y = (y - (owner // 2) % 4) % 4
    core = owner % 2
    near = jnp.where(core == 0, far_x, far_y)
    far = jnp.where(core == 0, far_y, far_x)
    return (((core ^ c) * 4 + far) * 4 + near) * BINS + within


def exchange_views(close, away, later):
    def step(value, r):
        return lax.ppermute(value, "view", [(v, v ^ r) for v in range(N_VIEW)])

    got = {r: step(away[r - 4 : r - 3], r) for r in (4, 5, 6, 7)}
    close, later = tie(close, later)
    got.update({r: step(close[r : r + 1], r) for r in (3, 2, 1)})
    return jnp.concatenate([close[0:1]] + [got[r] for r in range(1, N_VIEW)], axis=0), later


def place_of(view):
    return view ^ lax.axis_index("view")


def across_view(value):
    return lax.all_to_all(value, "view", split_axis=0, concat_axis=0, tiled=True)


def across_tile(value):
    return lax.all_to_all(value, "tile", split_axis=0, concat_axis=0, tiled=True)


def local(
    features,
    moment_first,
    moment_second,
    positions,
    scales,
    opacity,
    cameras_first,
    shift_first,
    lists_first,
    loads_first,
    target,
    owner_after,
    cameras_second,
    shift_second,
    lists_second,
    loads_second,
):
    positions = jnp.transpose(positions, (1, 0, 2))
    colors, screen, geometry = prep(cameras_first, owner_after, features, positions, scales, opacity)
    screen = across_tile(screen)
    own, screen = gather_plane(gather_line(colors), screen)
    w_first, token = weights(lists_first[0], loads_first[0], shift_first[0], screen, "weights_first")
    *own, token = tie(*own, token)
    slots = color_slots(lists_first[0], lists_first[0] % BINS) + token[0, 0]
    parts = first_render(slots, loads_first[0], w_first, target[0], swapped(own))
    line, geometry = scatter_far(parts, geometry)
    screen = screen_again(cameras_second[0], across_view(geometry))
    line, screen = tie(line, screen)
    screen = across_tile(screen)
    gradient = scatter_near(line)
    me = lax.axis_index("view").reshape(1)
    close, away, packed = adam(owner_after, me, gradient, features, moment_first, moment_second)
    colors, screen = exchange_views(close, away, screen)
    colors, packed = tie(colors, packed)
    w_second, token = weights(lists_second[0], loads_second[0], shift_second[0], screen, "weights_second")
    packed = across_view(packed)
    *own, token = tie(*gather_plane(gather_line(colors)), token)
    blocks = swapped(own)
    slots = color_slots(lists_second[0], place_of(lists_second[0] % BINS)) + token[0, 0]
    image = second_render(slots, loads_second[0], w_second, blocks)
    new_features, new_first, new_second = (packed[:, i * C : i * C + C] for i in range(3))
    return (image[None], new_features, new_first, new_second)


def solution(mesh):
    return jax.shard_map(
        local,
        mesh=mesh,
        in_specs=(
            P(("view", "tile"), None, None),
            P(("view", "tile"), None, None),
            P(("view", "tile"), None, None),
            P(("view", "tile"), None, None),
            P(("view", "tile"), None),
            P(("view", "tile"), None),
            P("view", None, None),
            P("view", "tile", None),
            P("view", "tile", None),
            P("view", "tile"),
            P("view", "tile", None, None),
            P(("view", "tile")),
            P("view", None, None),
            P("view", "tile", None),
            P("view", "tile", None),
            P("view", "tile"),
        ),
        out_specs=(
            P("view", "tile", None, None),
            P(("view", "tile"), None, None),
            P(("view", "tile"), None, None),
            P(("view", "tile"), None, None),
        ),
        check_vma=False,
    )
```

```python
import functools

import jax
import jax.numpy as jnp
from jax import lax
from jax.experimental import pallas as pl
from jax.experimental.pallas import tpu as pltpu
from jax.sharding import PartitionSpec as P

C = 64
GB = 128
PIX = 256
SIDE = 16
LBLK = 8
TILES = 16
BINS = 8
N_VIEW = 8
N_TILE = 32
ROWS = GB // 8

beta_first = 0.9
beta_second = 0.999
learn_rate = 0.05
adam_epsilon = 1e-08
bias_first = 1.0 - 0.9**10
bias_second = 1.0 - 0.999**10

VM = pl.BlockSpec(memory_space=pltpu.VMEM)
SM = pl.BlockSpec(memory_space=pltpu.SMEM)
ANY = pl.BlockSpec(memory_space=pl.ANY)
GROUP = 8
LATER = 4
WEIGHTS_MIB = 60
RENDER_MIB = 34
SECOND_MIB = 48
LOG2E = 1.4426950408889634
f32 = jnp.float32
bf16 = jnp.bfloat16


def params(mib, **more):
    return pltpu.CompilerParams(vmem_limit_bytes=mib * 1024 * 1024, **more)


def onehot(inverse):
    row = lax.broadcasted_iota(jnp.int32, (GB, GB), 0)
    col = lax.broadcasted_iota(jnp.int32, (GB, GB), 1)
    if inverse:
        row, col = col, row
    return jnp.where(col == (row % ROWS) * 8 + row // ROWS, 1.0, 0.0).astype(bf16)


def reorder(values, inverse):
    return jnp.dot(values, onehot(inverse), preferred_element_type=f32)


def reorder_wide(values, inverse):
    high = values.astype(bf16)
    rest = values - high.astype(f32)
    middle = rest.astype(bf16)
    low = (rest - middle.astype(f32)).astype(bf16)
    return (reorder(high, inverse) + reorder(middle, inverse)) + reorder(low, inverse)


def project_rows(p0, p1, p2, scales, opacity, camera):
    mean_x = camera[0, 0] * p0 + camera[0, 1] * p1 + camera[0, 2] * p2 + camera[0, 3]
    mean_y = camera[1, 0] * p0 + camera[1, 1] * p1 + camera[1, 2] * p2 + camera[1, 3]
    falloff = 0.5 / (scales * scales)
    opaque = 1.0 / (1.0 + jnp.exp(-opacity))
    stack = jnp.concatenate([mean_x, mean_y, falloff, opaque], axis=0)
    return reorder(stack.astype(bf16), False)


def screen_rows(stack):
    rows = [stack[k * BINS + b : k * BINS + b + 1] for b in range(BINS) for k in range(4)]
    return jnp.concatenate(rows, axis=0).astype(bf16)


def spread(stack, screen):
    rows = screen_rows(stack)
    for t in range(N_TILE):
        screen[t] = rows


def fetch(pairs, sems):
    copies = [pltpu.make_async_copy(source, to, sems.at[i]) for i, (source, to) in enumerate(pairs)]
    for copy in copies:
        copy.start()
    return copies


def prep_kernel(camera_hbm, owner_hbm, feat_hbm, pos_hbm, scales_hbm, opacity_hbm, colors, screen, geometry, *scratch):
    camera, owner, feat, pos, scales, opacity, sems = scratch
    copies = fetch(
        [
            (camera_hbm, camera),
            (owner_hbm, owner),
            (feat_hbm, feat),
            (pos_hbm, pos),
            (scales_hbm, scales),
            (opacity_hbm, opacity),
        ],
        sems,
    )
    for copy in copies:
        copy.wait()
    flat = feat[...].reshape(BINS * C, GB).astype(bf16)
    colors[...] = reorder(flat, False).astype(bf16).reshape(BINS, C, GB)
    stack = project_rows(pos[0], pos[1], pos[2], scales[...], opacity[...], camera.at[0])
    spread(stack, screen)
    for s in range(BINS):
        rows = [pos[k, s : s + 1] for k in range(3)]
        rows += [scales[s : s + 1], opacity[s : s + 1], jnp.zeros((3, GB), f32)]
        geometry[owner[s]] = jnp.concatenate(rows, axis=0)


def prep(camera, owner, feat, pos, scales, opacity):
    return pl.pallas_call(
        prep_kernel,
        out_shape=(
            jax.ShapeDtypeStruct((BINS, C, GB), bf16),
            jax.ShapeDtypeStruct((N_TILE, BINS * 4, GB), bf16),
            jax.ShapeDtypeStruct((N_VIEW, 8, GB), f32),
        ),
        in_specs=[ANY] * 6,
        out_specs=(VM, VM, VM),
        scratch_shapes=[
            pltpu.SMEM((1, 2, 4), f32),
            pltpu.SMEM((BINS,), jnp.int32),
            pltpu.VMEM((BINS, C, GB), f32),
            pltpu.VMEM((3, BINS, GB), f32),
            pltpu.VMEM((BINS, GB), f32),
            pltpu.VMEM((BINS, GB), f32),
            pltpu.SemaphoreType.DMA((6,)),
        ],
        compiler_params=params(60),
        name="prep",
    )(camera, owner, feat, pos, scales, opacity)


def screen_kernel(camera, geometry, screen):
    rows = [jnp.concatenate([geometry[b, k : k + 1] for b in range(BINS)], axis=0) for k in range(5)]
    spread(project_rows(*rows, camera), screen)


def screen_again(camera, geometry):
    return pl.pallas_call(
        screen_kernel,
        out_shape=jax.ShapeDtypeStruct((N_TILE, BINS * 4, GB), bf16),
        in_specs=[SM, VM],
        out_specs=VM,
        compiler_params=params(8),
        name="screen_again",
    )(camera, geometry)


def weights_kernel(lists_hbm, loads_hbm, shift_hbm, screen_hbm, out_hbm, token, *scratch):
    lists, loads, shift, screen, bins, out, work, sem, sems = scratch
    copies = fetch([(lists_hbm, lists), (loads_hbm, loads), (shift_hbm, shift), (screen_hbm, screen)], sems)
    token[...] = jnp.zeros((8, GB), jnp.int32)
    row = lax.broadcasted_iota(jnp.int32, (8, GB), 0)
    lane = lax.broadcasted_iota(jnp.int32, (8, GB), 1)
    pixel_x = (lane % SIDE).astype(f32) + 0.5
    pixel_y = (lane // SIDE).astype(f32) + 0.5
    for copy in copies:
        copy.wait()

    def widen(t, unused):
        rows = screen[t].astype(f32)
        for i in range(BINS // 2):
            two = rows[8 * i : 8 * i + 8]
            bins[t * BINS + 2 * i] = two
            bins[t * BINS + 2 * i + 1] = pltpu.roll(two, 4, 0)
        return unused

    lax.fori_loop(0, N_TILE, widen, 0, unroll=4)
    source = lax.broadcasted_iota(jnp.int32, (GROUP * 8, 4 * GB), 0)
    wanted = lax.broadcasted_iota(jnp.int32, (GROUP * 8, 4 * GB), 1) // GB

    def one(wide, place_x, place_y):
        running = [jnp.ones((8, GB), f32) for half in range(2)]
        parts = [[], []]
        for v in range(ROWS):
            some = wide[v * 8 : v * 8 + 8]
            mean_x, mean_y, fall, opaque = (some[:, k * GB : k * GB + GB] for k in range(4))
            fall = fall * -LOG2E
            delta_x = place_x - mean_x
            along_x = delta_x * delta_x * fall
            for half in range(2):
                delta_y = place_y[half] - mean_y
                part = opaque * jnp.exp2(along_x + delta_y * delta_y * fall) * running[half]
                parts[half].append(part)
                running[half] = running[half] - part
        before, after = [], []
        for total in running:
            for step in (1, 2, 4):
                total = total * jnp.where(row >= step, pltpu.roll(total, step, 0), 1.0)
            before.append(jnp.where(row >= 1, pltpu.roll(total, 1, 0), 1.0))
            after.append(jnp.broadcast_to(total[7:8], (8, GB)))
        return parts, before, after

    def plan(tile, state):
        count, spare = state
        live = loads[tile]
        for q in range(LBLK):
            work[count + q] = tile * LBLK + q
        return count + live, jnp.where(live < LBLK, tile * LBLK + LBLK - 1, spare)

    count, spare = lax.fori_loop(0, TILES, plan, (0, 0))
    for k in range(GROUP):
        work[count + k] = spare

    def leave(item):
        return pltpu.make_async_copy(out.at[item], out_hbm.at[item // LBLK, item % LBLK], sem)

    def group(step, carried):
        items = [work[step * GROUP + k] for k in range(GROUP)]
        done, values = [], []
        for item in items:
            tile, q = item // LBLK, item % LBLK
            alive = jnp.where(q < loads[tile], 1.0, 0.0)
            value = bins[lists[q, tile]]
            values.append(jnp.where(row == 3, value * alive, value))
        columns = jnp.concatenate(values, axis=0).T.astype(bf16)
        for k, item in enumerate(items):
            tile = item // LBLK
            pick = jnp.where(source == wanted + 8 * k, 1.0, 0.0).astype(bf16)
            wide = jnp.dot(columns, pick, preferred_element_type=f32)
            place_x = pixel_x + shift[0, tile]
            place_y = [pixel_y + shift[1, tile] + 8.0 * half for half in range(2)]
            done.append(one(wide, place_x, place_y))
        for item, (parts, before, after) in zip(items, done):
            fresh = item % LBLK == 0
            carried = [jnp.where(fresh, 1.0, value) for value in carried]
            for half in range(2):
                scale = carried[half] * before[half]
                rows = [part * scale for part in parts[half]]
                out[item, :, half * GB : half * GB + GB] = jnp.concatenate(rows, axis=0).astype(bf16)
            carried = [carried[half] * after[half] for half in range(2)]
        for k, item in enumerate(items):

            @pl.when(step * GROUP + k < count)
            def _():
                leave(item).start()

        return tuple(carried)

    lax.fori_loop(0, (count + GROUP - 1) // GROUP, group, (jnp.ones((8, GB), f32),) * 2)

    def arrived(i, unused):
        leave(0).wait()
        return unused

    lax.fori_loop(0, count, arrived, 0)


def weights(lists, loads, shift, screen, name):
    return pl.pallas_call(
        weights_kernel,
        out_shape=(jax.ShapeDtypeStruct((TILES, LBLK, GB, PIX), bf16), jax.ShapeDtypeStruct((8, GB), jnp.int32)),
        in_specs=[ANY] * 4,
        out_specs=(ANY, VM),
        scratch_shapes=[
            pltpu.SMEM((LBLK, TILES), jnp.int32),
            pltpu.SMEM((TILES,), jnp.int32),
            pltpu.SMEM((2, TILES), f32),
            pltpu.VMEM((N_TILE, BINS * 4, GB), bf16),
            pltpu.VMEM((N_TILE * BINS, 8, GB), f32),
            pltpu.VMEM((TILES * LBLK, GB, PIX), bf16),
            pltpu.SMEM((TILES * LBLK + LBLK,), jnp.int32),
            pltpu.SemaphoreType.DMA,
            pltpu.SemaphoreType.DMA((4,)),
        ],
        compiler_params=params(WEIGHTS_MIB),
        cost_estimate=pl.CostEstimate(
            flops=TILES * LBLK * GB * PIX * 14, bytes_accessed=10_000_000, transcendentals=TILES * LBLK * GB * PIX
        ),
        name=name,
    )(lists.T, loads, shift.T, screen)


def load_colors(blocks, colors, sems):
    return fetch([(block, colors.at[pl.ds(i * 32, 32)]) for i, block in enumerate(blocks)], sems)


def fetch_weights(loads, w_hbm, w, sems):
    def tile_start(tile, unused):
        for q in range(LBLK):

            @pl.when(q < loads[tile])
            def _():
                pltpu.make_async_copy(w_hbm.at[tile, q], w.at[tile, q], sems.at[tile]).start()

        return unused

    lax.fori_loop(0, TILES, tile_start, 0)


def over_tiles(loads, w_hbm, w, sems, body):
    def each_tile(tile, unused):
        live = loads[tile]
        for size in range(1, LBLK + 1):

            @pl.when(live == size)
            def _():
                pltpu.make_async_copy(
                    w_hbm.at[tile, pl.ds(0, size)], w.at[tile, pl.ds(0, size)], sems.at[tile]
                ).wait()
                body(tile, w[tile, :size].reshape(size * GB, PIX), size)

        return unused

    lax.fori_loop(0, TILES, each_tile, 0)


def picture(slots, tile, w, size, colors):
    row = jnp.concatenate([colors[slots[tile, q]] for q in range(size)], axis=1)
    return jnp.dot(row, w, preferred_element_type=f32)


def first_kernel(slots, loads, w_hbm, target_hbm, *rest):
    blocks, outs, (colors, w, target, total, sems, w_sems, t_sem) = rest[:8], rest[8:16], rest[16:]
    copies = load_colors(blocks, colors, sems) + fetch([(target_hbm, target)], t_sem)
    fetch_weights(loads, w_hbm, w, w_sems)

    def clear(i, unused):
        total[pl.ds(i * 8, 8)] = jnp.zeros((8, C, GB), f32)
        return unused

    lax.fori_loop(0, N_TILE, clear, 0)
    for copy in copies:
        copy.wait()

    def body(tile, w, size):
        residual = (picture(slots, tile, w, size, colors) - target[tile].astype(f32)).astype(bf16)
        pieces = lax.dot_general(residual, w, (((1,), (1,)), ((), ())), preferred_element_type=f32)
        for q in range(size):
            slot = slots[tile, q]
            total[slot] = total[slot] + pieces[:, q * GB : q * GB + GB]

    over_tiles(loads, w_hbm, w, w_sems, body)
    copies = fetch([(total.at[pl.ds(i * 32, 32)], out) for i, out in enumerate(outs)], sems)
    for copy in copies:
        copy.wait()


def first_render(slots, loads, w, target, blocks):
    return pl.pallas_call(
        first_kernel,
        out_shape=(jax.ShapeDtypeStruct((32, C, GB), f32),) * 8,
        in_specs=[SM, SM, ANY, ANY] + [ANY] * 8,
        out_specs=(ANY,) * 8,
        scratch_shapes=[
            pltpu.VMEM((N_TILE * BINS, C, GB), bf16),
            pltpu.VMEM((TILES, LBLK, GB, PIX), bf16),
            pltpu.VMEM((TILES, C, PIX), bf16),
            pltpu.VMEM((N_TILE * BINS, C, GB), f32),
            pltpu.SemaphoreType.DMA((8,)),
            pltpu.SemaphoreType.DMA((TILES,)),
            pltpu.SemaphoreType.DMA((1,)),
        ],
        compiler_params=params(RENDER_MIB),
        cost_estimate=pl.CostEstimate(flops=TILES * LBLK * C * GB * PIX * 4, bytes_accessed=25_000_000, transcendentals=0),
        name="first_render",
    )(slots, loads, w, target, *blocks)


def second_kernel(slots, loads, w_hbm, *rest):
    blocks, image, (colors, w, sems, w_sems) = rest[:8], rest[8], rest[9:]
    copies = load_colors(blocks, colors, sems)
    fetch_weights(loads, w_hbm, w, w_sems)
    for copy in copies:
        copy.wait()

    def body(tile, w, size):
        image[tile] = picture(slots, tile, w, size, colors)

    over_tiles(loads, w_hbm, w, w_sems, body)


def second_render(slots, loads, w, blocks):
    return pl.pallas_call(
        second_kernel,
        out_shape=jax.ShapeDtypeStruct((TILES, C, PIX), f32),
        in_specs=[SM, SM, ANY] + [ANY] * 8,
        out_specs=VM,
        scratch_shapes=[
            pltpu.VMEM((N_TILE * BINS, C, GB), bf16),
            pltpu.VMEM((TILES, LBLK, GB, PIX), bf16),
            pltpu.SemaphoreType.DMA((8,)),
            pltpu.SemaphoreType.DMA((TILES,)),
        ],
        compiler_params=params(SECOND_MIB),
        cost_estimate=pl.CostEstimate(flops=TILES * LBLK * C * GB * PIX * 2, bytes_accessed=14_000_000, transcendentals=0),
        name="second_render",
    )(slots, loads, w, *blocks)


def adam_kernel(owner, me, gradient, feat, m1, m2, *rest):
    outs, packed, colors = rest[:N_VIEW], rest[N_VIEW], rest[N_VIEW + 1]
    g = reorder_wide(gradient[...].reshape(BINS * C, GB), True).reshape(BINS, C, GB)
    first_new = beta_first * m1[...] + (1.0 - beta_first) * g
    second_new = beta_second * m2[...] + (1.0 - beta_second) * g * g
    stepped = feat[...] - learn_rate * (first_new / bias_first) / (jnp.sqrt(second_new / bias_second) + adam_epsilon)
    flat = stepped.reshape(BINS * C, GB).astype(bf16)
    sent = reorder(flat, False).astype(bf16).reshape(BINS, C, GB)
    for s in range(BINS):
        w = owner[s]
        colors[w ^ me[0]] = sent[s]
        packed[w, 0:C] = stepped[s]
        packed[w, C : 2 * C] = first_new[s]
        packed[w, 2 * C : 3 * C] = second_new[s]
    for r, out in enumerate(outs):
        out[...] = colors[r : r + 1]


def adam(owner, me, gradient, feat, m1, m2):
    return pl.pallas_call(
        adam_kernel,
        out_shape=(
            *(jax.ShapeDtypeStruct((1, C, GB), bf16),) * N_VIEW,
            jax.ShapeDtypeStruct((N_VIEW, 3 * C, GB), f32),
        ),
        in_specs=[SM, SM, VM, VM, VM, VM],
        out_specs=(VM,) * (N_VIEW + 1),
        scratch_shapes=[pltpu.VMEM((N_VIEW, C, GB), bf16)],
        compiler_params=params(16),
        name="adam",
    )(owner, me, gradient, feat, m1, m2)


def device(x, y, c):
    return ((x % 4) * 4 + y % 4) * 2 + c


def shift_by(value, level, k):
    pairs = []
    for x in range(4):
        for y in range(4):
            for c in range(2):
                dx, dy = (k, 0) if c == level else (0, k)
                pairs.append((device(x, y, c), device(x + dx, y + dy, c)))
    return lax.ppermute(value, "tile", pairs)


def swap_core(value):
    pairs = [(t, t ^ 1) for t in range(N_TILE)]
    return lax.ppermute(value, "tile", pairs)


ORDER = (2, 1, 3)


def tie(*values):
    return lax.optimization_barrier(values)


def gather_line(colors):
    near = {0: colors}
    for k in ORDER:
        near[k] = shift_by(colors, 0, k)
    return jnp.concatenate([near[k] for k in range(4)], axis=0)


def gather_plane(line, later=None):
    plane = {0: line}
    for k in ORDER:
        if later is not None and k == ORDER[-1]:
            line, later = tie(line, later)
        plane[k] = shift_by(line, 1, k)
    own = [plane[k] for k in range(4)]
    return own if later is None else (own, later)


def swapped(own):
    return list(own) + [swap_core(block) for block in own]


def scatter_far(parts, later):
    half16 = jnp.float16
    sent = {}
    for k in ORDER:
        sent[k] = (parts[k] + swap_core(parts[4 + k])).astype(half16)
    line = parts[0] + swap_core(parts[4])
    sent[3], later = tie(sent[3], later)
    for k in ORDER:
        line = line + shift_by(sent[k], 1, -k).astype(f32)
    return line, later


def scatter_near(line):
    half16 = jnp.float16
    total = line[0:BINS]
    for k in ORDER:
        total = total + shift_by(line[k * BINS : (k + 1) * BINS].astype(half16), 0, -k).astype(f32)
    return total


def color_slots(lists, within):
    me = lax.axis_index("tile")
    x, y, c = me // 8, (me // 2) % 4, me % 2
    owner = lists // BINS
    far_x = (x - owner // 8) % 4
    far_y = (y - (owner // 2) % 4) % 4
    core = owner % 2
    near = jnp.where(core == 0, far_x, far_y)
    far = jnp.where(core == 0, far_y, far_x)
    return (((core ^ c) * 4 + far) * 4 + near) * BINS + within


def exchange_views(colors, later):
    got = {0: colors[0]}
    for i, r in enumerate((4, 5, 3, 6, 2, 7, 1)):
        value = colors[r]
        if i == LATER:
            value, later = tie(value, later)
        got[r] = lax.ppermute(value, "view", [(v, v ^ r) for v in range(N_VIEW)])
    return jnp.concatenate([got[r] for r in range(N_VIEW)], axis=0), later


def place_of(view):
    return view ^ lax.axis_index("view")


def across_view(value):
    return lax.all_to_all(value, "view", split_axis=0, concat_axis=0, tiled=True)


def across_tile(value):
    return lax.all_to_all(value, "tile", split_axis=0, concat_axis=0, tiled=True)


def local(
    features,
    moment_first,
    moment_second,
    positions,
    scales,
    opacity,
    cameras_first,
    shift_first,
    lists_first,
    loads_first,
    target,
    owner_after,
    cameras_second,
    shift_second,
    lists_second,
    loads_second,
):
    positions = jnp.transpose(positions, (1, 0, 2))
    colors, screen, geometry = prep(cameras_first, owner_after, features, positions, scales, opacity)
    screen = across_tile(screen)
    own, screen = gather_plane(gather_line(colors), screen)
    w_first, token = weights(lists_first[0], loads_first[0], shift_first[0], screen, "weights_first")
    *own, token = tie(*own, token)
    slots = color_slots(lists_first[0], lists_first[0] % BINS) + token[0, 0]
    parts = first_render(slots, loads_first[0], w_first, target[0], swapped(own))
    line, geometry = scatter_far(parts, geometry)
    screen = screen_again(cameras_second[0], across_view(geometry))
    line, screen = tie(line, screen)
    screen = across_tile(screen)
    gradient = scatter_near(line)
    me = lax.axis_index("view").reshape(1)
    *colors, packed = adam(owner_after, me, gradient, features, moment_first, moment_second)
    colors, screen = exchange_views(colors, screen)
    colors, packed = tie(colors, packed)
    w_second, token = weights(lists_second[0], loads_second[0], shift_second[0], screen, "weights_second")
    packed = across_view(packed)
    *own, token = tie(*gather_plane(gather_line(colors)), token)
    blocks = swapped(own)
    slots = color_slots(lists_second[0], place_of(lists_second[0] % BINS)) + token[0, 0]
    image = second_render(slots, loads_second[0], w_second, blocks)
    new_features, new_first, new_second = (packed[:, i * C : i * C + C] for i in range(3))
    return (image[None], new_features, new_first, new_second)


def solution(mesh):
    return jax.shard_map(
        local,
        mesh=mesh,
        in_specs=(
            P(("view", "tile"), None, None),
            P(("view", "tile"), None, None),
            P(("view", "tile"), None, None),
            P(("view", "tile"), None, None),
            P(("view", "tile"), None),
            P(("view", "tile"), None),
            P("view", None, None),
            P("view", "tile", None),
            P("view", "tile", None),
            P("view", "tile"),
            P("view", "tile", None, None),
            P(("view", "tile")),
            P("view", None, None),
            P("view", "tile", None),
            P("view", "tile", None),
            P("view", "tile"),
        ),
        out_specs=(
            P("view", "tile", None, None),
            P(("view", "tile"), None, None),
            P(("view", "tile"), None, None),
            P(("view", "tile"), None, None),
        ),
        check_vma=False,
    )
```

```python
import functools

import jax
import jax.numpy as jnp
from jax import lax
from jax.experimental import pallas as pl
from jax.experimental.pallas import tpu as pltpu
from jax.sharding import PartitionSpec as P

C = 64
GB = 128
PIX = 256
SIDE = 16
LBLK = 8
TILES = 16
BINS = 8
N_VIEW = 8
N_TILE = 32
ROWS = GB // 8

beta_first = 0.9
beta_second = 0.999
learn_rate = 0.05
adam_epsilon = 1e-08
bias_first = 1.0 - 0.9**10
bias_second = 1.0 - 0.999**10

VM = pl.BlockSpec(memory_space=pltpu.VMEM)
SM = pl.BlockSpec(memory_space=pltpu.SMEM)
ANY = pl.BlockSpec(memory_space=pl.ANY)
GROUP = 8
LATER = 4
WEIGHTS_MIB = 60
RENDER_MIB = 34
SECOND_MIB = 48
LOG2E = 1.4426950408889634
f32 = jnp.float32
bf16 = jnp.bfloat16


def params(mib, **more):
    return pltpu.CompilerParams(vmem_limit_bytes=mib * 1024 * 1024, **more)


def onehot(inverse):
    row = lax.broadcasted_iota(jnp.int32, (GB, GB), 0)
    col = lax.broadcasted_iota(jnp.int32, (GB, GB), 1)
    if inverse:
        row, col = col, row
    return jnp.where(col == (row % ROWS) * 8 + row // ROWS, 1.0, 0.0).astype(bf16)


def reorder(values, inverse):
    return jnp.dot(values, onehot(inverse), preferred_element_type=f32)


def reorder_wide(values, inverse):
    high = values.astype(bf16)
    rest = values - high.astype(f32)
    middle = rest.astype(bf16)
    low = (rest - middle.astype(f32)).astype(bf16)
    return (reorder(high, inverse) + reorder(middle, inverse)) + reorder(low, inverse)


def project_rows(p0, p1, p2, scales, opacity, camera):
    mean_x = camera[0, 0] * p0 + camera[0, 1] * p1 + camera[0, 2] * p2 + camera[0, 3]
    mean_y = camera[1, 0] * p0 + camera[1, 1] * p1 + camera[1, 2] * p2 + camera[1, 3]
    falloff = 0.5 / (scales * scales)
    opaque = 1.0 / (1.0 + jnp.exp(-opacity))
    stack = jnp.concatenate([mean_x, mean_y, falloff, opaque], axis=0)
    return reorder(stack.astype(bf16), False)


def screen_rows(stack):
    rows = [stack[k * BINS + b : k * BINS + b + 1] for b in range(BINS) for k in range(4)]
    return jnp.concatenate(rows, axis=0).astype(bf16)


def spread(stack, screen):
    rows = screen_rows(stack)
    for t in range(N_TILE):
        screen[t] = rows


def fetch(pairs, sems):
    copies = [pltpu.make_async_copy(source, to, sems.at[i]) for i, (source, to) in enumerate(pairs)]
    for copy in copies:
        copy.start()
    return copies


def prep_kernel(camera_hbm, owner_hbm, feat_hbm, pos_hbm, scales_hbm, opacity_hbm, colors, screen, geometry, *scratch):
    camera, owner, feat, pos, scales, opacity, sems = scratch
    copies = fetch(
        [
            (camera_hbm, camera),
            (owner_hbm, owner),
            (feat_hbm, feat),
            (pos_hbm, pos),
            (scales_hbm, scales),
            (opacity_hbm, opacity),
        ],
        sems,
    )
    for copy in copies:
        copy.wait()
    flat = feat[...].reshape(BINS * C, GB).astype(bf16)
    colors[...] = reorder(flat, False).astype(bf16).reshape(BINS, C, GB)
    stack = project_rows(pos[0], pos[1], pos[2], scales[...], opacity[...], camera.at[0])
    spread(stack, screen)
    for s in range(BINS):
        rows = [pos[k, s : s + 1] for k in range(3)]
        rows += [scales[s : s + 1], opacity[s : s + 1], jnp.zeros((3, GB), f32)]
        geometry[owner[s]] = jnp.concatenate(rows, axis=0)


def prep(camera, owner, feat, pos, scales, opacity):
    return pl.pallas_call(
        prep_kernel,
        out_shape=(
            jax.ShapeDtypeStruct((BINS, C, GB), bf16),
            jax.ShapeDtypeStruct((N_TILE, BINS * 4, GB), bf16),
            jax.ShapeDtypeStruct((N_VIEW, 8, GB), f32),
        ),
        in_specs=[ANY] * 6,
        out_specs=(VM, VM, VM),
        scratch_shapes=[
            pltpu.SMEM((1, 2, 4), f32),
            pltpu.SMEM((BINS,), jnp.int32),
            pltpu.VMEM((BINS, C, GB), f32),
            pltpu.VMEM((3, BINS, GB), f32),
            pltpu.VMEM((BINS, GB), f32),
            pltpu.VMEM((BINS, GB), f32),
            pltpu.SemaphoreType.DMA((6,)),
        ],
        compiler_params=params(60),
        name="prep",
    )(camera, owner, feat, pos, scales, opacity)


def screen_kernel(camera, geometry, screen):
    rows = [jnp.concatenate([geometry[b, k : k + 1] for b in range(BINS)], axis=0) for k in range(5)]
    spread(project_rows(*rows, camera), screen)


def screen_again(camera, geometry):
    return pl.pallas_call(
        screen_kernel,
        out_shape=jax.ShapeDtypeStruct((N_TILE, BINS * 4, GB), bf16),
        in_specs=[SM, VM],
        out_specs=VM,
        compiler_params=params(8),
        name="screen_again",
    )(camera, geometry)


def weights_kernel(lists_hbm, loads_hbm, shift_hbm, screen_hbm, out_hbm, token, *scratch):
    lists, loads, shift, screen, bins, out, work, sem, sems = scratch
    copies = fetch([(lists_hbm, lists), (loads_hbm, loads), (shift_hbm, shift), (screen_hbm, screen)], sems)
    token[...] = jnp.zeros((8, GB), jnp.int32)
    row = lax.broadcasted_iota(jnp.int32, (8, GB), 0)
    lane = lax.broadcasted_iota(jnp.int32, (8, GB), 1)
    pixel_x = (lane % SIDE).astype(f32) + 0.5
    pixel_y = (lane // SIDE).astype(f32) + 0.5
    for copy in copies:
        copy.wait()

    def widen(t, unused):
        rows = screen[t].astype(f32)
        for i in range(BINS // 2):
            two = rows[8 * i : 8 * i + 8]
            bins[t * BINS + 2 * i] = two
            bins[t * BINS + 2 * i + 1] = pltpu.roll(two, 4, 0)
        return unused

    lax.fori_loop(0, N_TILE, widen, 0, unroll=4)
    source = lax.broadcasted_iota(jnp.int32, (GROUP * 8, 4 * GB), 0)
    wanted = lax.broadcasted_iota(jnp.int32, (GROUP * 8, 4 * GB), 1) // GB

    def one(wide, place_x, place_y):
        running = [jnp.ones((8, GB), f32) for half in range(2)]
        parts = [[], []]
        for v in range(ROWS):
            some = wide[v * 8 : v * 8 + 8]
            mean_x, mean_y, fall, opaque = (some[:, k * GB : k * GB + GB] for k in range(4))
            fall = fall * -LOG2E
            delta_x = place_x - mean_x
            along_x = delta_x * delta_x * fall
            for half in range(2):
                delta_y = place_y[half] - mean_y
                part = opaque * jnp.exp2(along_x + delta_y * delta_y * fall) * running[half]
                parts[half].append(part)
                running[half] = running[half] - part
        before, after = [], []
        for total in running:
            for step in (1, 2, 4):
                total = total * jnp.where(row >= step, pltpu.roll(total, step, 0), 1.0)
            before.append(jnp.where(row >= 1, pltpu.roll(total, 1, 0), 1.0))
            after.append(jnp.broadcast_to(total[7:8], (8, GB)))
        return parts, before, after

    def plan(tile, state):
        count, spare = state
        live = loads[tile]
        for q in range(LBLK):
            work[count + q] = tile * LBLK + q
        return count + live, jnp.where(live < LBLK, tile * LBLK + LBLK - 1, spare)

    count, spare = lax.fori_loop(0, TILES, plan, (0, 0))
    for k in range(GROUP):
        work[count + k] = spare

    def leave(item):
        return pltpu.make_async_copy(out.at[item], out_hbm.at[item // LBLK, item % LBLK], sem)

    def group(step, carried):
        items = [work[step * GROUP + k] for k in range(GROUP)]
        done, values = [], []
        for item in items:
            tile, q = item // LBLK, item % LBLK
            alive = jnp.where(q < loads[tile], 1.0, 0.0)
            value = bins[lists[q, tile]]
            values.append(jnp.where(row == 3, value * alive, value))
        columns = jnp.concatenate(values, axis=0).T.astype(bf16)
        for k, item in enumerate(items):
            tile = item // LBLK
            pick = jnp.where(source == wanted + 8 * k, 1.0, 0.0).astype(bf16)
            wide = jnp.dot(columns, pick, preferred_element_type=f32)
            place_x = pixel_x + shift[0, tile]
            place_y = [pixel_y + shift[1, tile] + 8.0 * half for half in range(2)]
            done.append(one(wide, place_x, place_y))
        for item, (parts, before, after) in zip(items, done):
            fresh = item % LBLK == 0
            carried = [jnp.where(fresh, 1.0, value) for value in carried]
            for half in range(2):
                scale = carried[half] * before[half]
                rows = [part * scale for part in parts[half]]
                out[item, :, half * GB : half * GB + GB] = jnp.concatenate(rows, axis=0).astype(bf16)
            carried = [carried[half] * after[half] for half in range(2)]
        for k, item in enumerate(items):

            @pl.when(step * GROUP + k < count)
            def _():
                leave(item).start()

        return tuple(carried)

    lax.fori_loop(0, (count + GROUP - 1) // GROUP, group, (jnp.ones((8, GB), f32),) * 2)

    def arrived(i, unused):
        leave(0).wait()
        return unused

    lax.fori_loop(0, count, arrived, 0)


def weights(lists, loads, shift, screen, name):
    return pl.pallas_call(
        weights_kernel,
        out_shape=(jax.ShapeDtypeStruct((TILES, LBLK, GB, PIX), bf16), jax.ShapeDtypeStruct((8, GB), jnp.int32)),
        in_specs=[ANY] * 4,
        out_specs=(ANY, VM),
        scratch_shapes=[
            pltpu.SMEM((LBLK, TILES), jnp.int32),
            pltpu.SMEM((TILES,), jnp.int32),
            pltpu.SMEM((2, TILES), f32),
            pltpu.VMEM((N_TILE, BINS * 4, GB), bf16),
            pltpu.VMEM((N_TILE * BINS, 8, GB), f32),
            pltpu.VMEM((TILES * LBLK, GB, PIX), bf16),
            pltpu.SMEM((TILES * LBLK + LBLK,), jnp.int32),
            pltpu.SemaphoreType.DMA,
            pltpu.SemaphoreType.DMA((4,)),
        ],
        compiler_params=params(WEIGHTS_MIB),
        cost_estimate=pl.CostEstimate(
            flops=TILES * LBLK * GB * PIX * 14, bytes_accessed=10_000_000, transcendentals=TILES * LBLK * GB * PIX
        ),
        name=name,
    )(lists.T, loads, shift.T, screen)


def load_colors(blocks, colors, sems):
    return fetch([(block, colors.at[pl.ds(i * 32, 32)]) for i, block in enumerate(blocks)], sems)


def fetch_weights(loads, w_hbm, w, sems):
    def tile_start(tile, unused):
        for q in range(LBLK):

            @pl.when(q < loads[tile])
            def _():
                pltpu.make_async_copy(w_hbm.at[tile, q], w.at[tile, q], sems.at[tile]).start()

        return unused

    lax.fori_loop(0, TILES, tile_start, 0)


def over_tiles(loads, w_hbm, w, sems, body):
    def each_tile(tile, unused):
        live = loads[tile]
        for size in range(1, LBLK + 1):

            @pl.when(live == size)
            def _():
                pltpu.make_async_copy(
                    w_hbm.at[tile, pl.ds(0, size)], w.at[tile, pl.ds(0, size)], sems.at[tile]
                ).wait()
                body(tile, w[tile, :size].reshape(size * GB, PIX), size)

        return unused

    lax.fori_loop(0, TILES, each_tile, 0)


def picture(slots, tile, w, size, colors):
    row = jnp.concatenate([colors[slots[tile, q]] for q in range(size)], axis=1)
    return jnp.dot(row, w, preferred_element_type=f32)


def first_kernel(slots, loads, w_hbm, target_hbm, *rest):
    blocks, outs, (colors, w, target, total, sems, w_sems, t_sem) = rest[:8], rest[8:16], rest[16:]
    copies = load_colors(blocks, colors, sems) + fetch([(target_hbm, target)], t_sem)
    fetch_weights(loads, w_hbm, w, w_sems)

    def clear(i, unused):
        total[pl.ds(i * 8, 8)] = jnp.zeros((8, C, GB), f32)
        return unused

    lax.fori_loop(0, N_TILE, clear, 0)
    for copy in copies:
        copy.wait()

    def body(tile, w, size):
        residual = (picture(slots, tile, w, size, colors) - target[tile].astype(f32)).astype(bf16)
        pieces = lax.dot_general(residual, w, (((1,), (1,)), ((), ())), preferred_element_type=f32)
        for q in range(size):
            slot = slots[tile, q]
            total[slot] = total[slot] + pieces[:, q * GB : q * GB + GB]

    over_tiles(loads, w_hbm, w, w_sems, body)
    copies = fetch([(total.at[pl.ds(i * 32, 32)], out) for i, out in enumerate(outs)], sems)
    for copy in copies:
        copy.wait()


def first_render(slots, loads, w, target, blocks):
    return pl.pallas_call(
        first_kernel,
        out_shape=(jax.ShapeDtypeStruct((32, C, GB), f32),) * 8,
        in_specs=[SM, SM, ANY, ANY] + [ANY] * 8,
        out_specs=(ANY,) * 8,
        scratch_shapes=[
            pltpu.VMEM((N_TILE * BINS, C, GB), bf16),
            pltpu.VMEM((TILES, LBLK, GB, PIX), bf16),
            pltpu.VMEM((TILES, C, PIX), bf16),
            pltpu.VMEM((N_TILE * BINS, C, GB), f32),
            pltpu.SemaphoreType.DMA((8,)),
            pltpu.SemaphoreType.DMA((TILES,)),
            pltpu.SemaphoreType.DMA((1,)),
        ],
        compiler_params=params(RENDER_MIB),
        cost_estimate=pl.CostEstimate(flops=TILES * LBLK * C * GB * PIX * 4, bytes_accessed=25_000_000, transcendentals=0),
        name="first_render",
    )(slots, loads, w, target, *blocks)


def second_kernel(slots, loads, w_hbm, packed, *rest):
    blocks, image, news, (colors, w, sems, w_sems, n_sems) = rest[:8], rest[8], rest[9:12], rest[12:]
    copies = load_colors(blocks, colors, sems)
    fetch_weights(loads, w_hbm, w, w_sems)
    moves = fetch([(packed.at[:, pl.ds(i * C, C)], new) for i, new in enumerate(news)], n_sems)
    for copy in copies:
        copy.wait()

    def body(tile, w, size):
        image[tile] = picture(slots, tile, w, size, colors)

    over_tiles(loads, w_hbm, w, w_sems, body)
    for move in moves:
        move.wait()


def second_render(slots, loads, w, packed, blocks):
    wide = jax.ShapeDtypeStruct((BINS, C, GB), f32)
    return pl.pallas_call(
        second_kernel,
        out_shape=(jax.ShapeDtypeStruct((TILES, C, PIX), f32), wide, wide, wide),
        in_specs=[SM, SM, ANY, ANY] + [ANY] * 8,
        out_specs=(VM, ANY, ANY, ANY),
        scratch_shapes=[
            pltpu.VMEM((N_TILE * BINS, C, GB), bf16),
            pltpu.VMEM((TILES, LBLK, GB, PIX), bf16),
            pltpu.SemaphoreType.DMA((8,)),
            pltpu.SemaphoreType.DMA((TILES,)),
            pltpu.SemaphoreType.DMA((3,)),
        ],
        compiler_params=params(SECOND_MIB),
        cost_estimate=pl.CostEstimate(flops=TILES * LBLK * C * GB * PIX * 2, bytes_accessed=14_000_000, transcendentals=0),
        name="second_render",
    )(slots, loads, w, packed, *blocks)


def adam_kernel(owner, me, gradient, feat, m1, m2, *rest):
    outs, packed, colors = rest[:N_VIEW], rest[N_VIEW], rest[N_VIEW + 1]
    g = reorder_wide(gradient[...].reshape(BINS * C, GB), True).reshape(BINS, C, GB)
    first_new = beta_first * m1[...] + (1.0 - beta_first) * g
    second_new = beta_second * m2[...] + (1.0 - beta_second) * g * g
    stepped = feat[...] - learn_rate * (first_new / bias_first) / (jnp.sqrt(second_new / bias_second) + adam_epsilon)
    flat = stepped.reshape(BINS * C, GB).astype(bf16)
    sent = reorder(flat, False).astype(bf16).reshape(BINS, C, GB)
    for s in range(BINS):
        w = owner[s]
        colors[w ^ me[0]] = sent[s]
        packed[w, 0:C] = stepped[s]
        packed[w, C : 2 * C] = first_new[s]
        packed[w, 2 * C : 3 * C] = second_new[s]
    for r, out in enumerate(outs):
        out[...] = colors[r : r + 1]


def adam(owner, me, gradient, feat, m1, m2):
    return pl.pallas_call(
        adam_kernel,
        out_shape=(
            *(jax.ShapeDtypeStruct((1, C, GB), bf16),) * N_VIEW,
            jax.ShapeDtypeStruct((N_VIEW, 3 * C, GB), f32),
        ),
        in_specs=[SM, SM, VM, VM, VM, VM],
        out_specs=(VM,) * (N_VIEW + 1),
        scratch_shapes=[pltpu.VMEM((N_VIEW, C, GB), bf16)],
        compiler_params=params(16),
        name="adam",
    )(owner, me, gradient, feat, m1, m2)


def device(x, y, c):
    return ((x % 4) * 4 + y % 4) * 2 + c


def shift_by(value, level, k):
    pairs = []
    for x in range(4):
        for y in range(4):
            for c in range(2):
                dx, dy = (k, 0) if c == level else (0, k)
                pairs.append((device(x, y, c), device(x + dx, y + dy, c)))
    return lax.ppermute(value, "tile", pairs)


def swap_core(value):
    pairs = [(t, t ^ 1) for t in range(N_TILE)]
    return lax.ppermute(value, "tile", pairs)


ORDER = (2, 1, 3)


def tie(*values):
    return lax.optimization_barrier(values)


def gather_line(colors):
    near = {0: colors}
    for k in ORDER:
        near[k] = shift_by(colors, 0, k)
    return jnp.concatenate([near[k] for k in range(4)], axis=0)


def gather_plane(line, later=None):
    plane = {0: line}
    for k in ORDER:
        if later is not None and k == ORDER[-1]:
            line, later = tie(line, later)
        plane[k] = shift_by(line, 1, k)
    own = [plane[k] for k in range(4)]
    return own if later is None else (own, later)


def swapped(own):
    return list(own) + [swap_core(block) for block in own]


def scatter_far(parts, later):
    half16 = jnp.float16
    sent = {}
    for k in ORDER:
        sent[k] = (parts[k] + swap_core(parts[4 + k])).astype(half16)
    line = parts[0] + swap_core(parts[4])
    sent[3], later = tie(sent[3], later)
    for k in ORDER:
        line = line + shift_by(sent[k], 1, -k).astype(f32)
    return line, later


def scatter_near(line):
    half16 = jnp.float16
    total = line[0:BINS]
    for k in ORDER:
        total = total + shift_by(line[k * BINS : (k + 1) * BINS].astype(half16), 0, -k).astype(f32)
    return total


def color_slots(lists, within):
    me = lax.axis_index("tile")
    x, y, c = me // 8, (me // 2) % 4, me % 2
    owner = lists // BINS
    far_x = (x - owner // 8) % 4
    far_y = (y - (owner // 2) % 4) % 4
    core = owner % 2
    near = jnp.where(core == 0, far_x, far_y)
    far = jnp.where(core == 0, far_y, far_x)
    return (((core ^ c) * 4 + far) * 4 + near) * BINS + within


def exchange_views(colors, later):
    got = {0: colors[0]}
    for i, r in enumerate((4, 5, 3, 6, 2, 7, 1)):
        value = colors[r]
        if i == LATER:
            value, later = tie(value, later)
        got[r] = lax.ppermute(value, "view", [(v, v ^ r) for v in range(N_VIEW)])
    return jnp.concatenate([got[r] for r in range(N_VIEW)], axis=0), later


def place_of(view):
    return view ^ lax.axis_index("view")


def across_view(value):
    return lax.all_to_all(value, "view", split_axis=0, concat_axis=0, tiled=True)


def across_tile(value):
    return lax.all_to_all(value, "tile", split_axis=0, concat_axis=0, tiled=True)


def local(
    features,
    moment_first,
    moment_second,
    positions,
    scales,
    opacity,
    cameras_first,
    shift_first,
    lists_first,
    loads_first,
    target,
    owner_after,
    cameras_second,
    shift_second,
    lists_second,
    loads_second,
):
    positions = jnp.transpose(positions, (1, 0, 2))
    colors, screen, geometry = prep(cameras_first, owner_after, features, positions, scales, opacity)
    screen = across_tile(screen)
    own, screen = gather_plane(gather_line(colors), screen)
    w_first, token = weights(lists_first[0], loads_first[0], shift_first[0], screen, "weights_first")
    line, *own = own
    *own, token = tie(*own, token)
    slots = color_slots(lists_first[0], lists_first[0] % BINS) + token[0, 0]
    parts = first_render(slots, loads_first[0], w_first, target[0], swapped([line] + own))
    line, geometry = scatter_far(parts, geometry)
    screen = screen_again(cameras_second[0], across_view(geometry))
    line, screen = tie(line, screen)
    screen = across_tile(screen)
    gradient = scatter_near(line)
    me = lax.axis_index("view").reshape(1)
    *colors, packed = adam(owner_after, me, gradient, features, moment_first, moment_second)
    colors, screen = exchange_views(colors, screen)
    colors, packed = tie(colors, packed)
    w_second, token = weights(lists_second[0], loads_second[0], shift_second[0], screen, "weights_second")
    packed = across_view(packed)
    line, *own = gather_plane(gather_line(colors))
    *own, token = tie(*own, token)
    blocks = swapped([line] + own)
    slots = color_slots(lists_second[0], place_of(lists_second[0] % BINS)) + token[0, 0]
    image, new_features, new_first, new_second = second_render(
        slots, loads_second[0], w_second, packed, blocks
    )
    return (image[None], new_features, new_first, new_second)


def solution(mesh):
    return jax.shard_map(
        local,
        mesh=mesh,
        in_specs=(
            P(("view", "tile"), None, None),
            P(("view", "tile"), None, None),
            P(("view", "tile"), None, None),
            P(("view", "tile"), None, None),
            P(("view", "tile"), None),
            P(("view", "tile"), None),
            P("view", None, None),
            P("view", "tile", None),
            P("view", "tile", None),
            P("view", "tile"),
            P("view", "tile", None, None),
            P(("view", "tile")),
            P("view", None, None),
            P("view", "tile", None),
            P("view", "tile", None),
            P("view", "tile"),
        ),
        out_specs=(
            P("view", "tile", None, None),
            P(("view", "tile"), None, None),
            P(("view", "tile"), None, None),
            P(("view", "tile"), None, None),
        ),
        check_vma=False,
    )
```

```python
import functools

import jax
import jax.numpy as jnp
from jax import lax
from jax.experimental import pallas as pl
from jax.experimental.pallas import tpu as pltpu
from jax.sharding import PartitionSpec as P

C = 64
GB = 128
PIX = 256
SIDE = 16
LBLK = 8
TILES = 16
BINS = 8
N_VIEW = 8
N_TILE = 32
ROWS = GB // 8

beta_first = 0.9
beta_second = 0.999
learn_rate = 0.05
adam_epsilon = 1e-08
bias_first = 1.0 - 0.9**10
bias_second = 1.0 - 0.999**10

VM = pl.BlockSpec(memory_space=pltpu.VMEM)
SM = pl.BlockSpec(memory_space=pltpu.SMEM)
ANY = pl.BlockSpec(memory_space=pl.ANY)
GROUP = 8
LATER = 4
WEIGHTS_MIB = 60
RENDER_MIB = 34
SECOND_MIB = 48
LOG2E = 1.4426950408889634
f32 = jnp.float32
bf16 = jnp.bfloat16


def params(mib, **more):
    return pltpu.CompilerParams(vmem_limit_bytes=mib * 1024 * 1024, **more)


def onehot(inverse):
    row = lax.broadcasted_iota(jnp.int32, (GB, GB), 0)
    col = lax.broadcasted_iota(jnp.int32, (GB, GB), 1)
    if inverse:
        row, col = col, row
    return jnp.where(col == (row % ROWS) * 8 + row // ROWS, 1.0, 0.0).astype(bf16)


def reorder(values, inverse):
    return jnp.dot(values, onehot(inverse), preferred_element_type=f32)


def reorder_wide(values, inverse):
    high = values.astype(bf16)
    rest = values - high.astype(f32)
    middle = rest.astype(bf16)
    low = (rest - middle.astype(f32)).astype(bf16)
    return (reorder(high, inverse) + reorder(middle, inverse)) + reorder(low, inverse)


def project_rows(p0, p1, p2, scales, opacity, camera):
    mean_x = camera[0, 0] * p0 + camera[0, 1] * p1 + camera[0, 2] * p2 + camera[0, 3]
    mean_y = camera[1, 0] * p0 + camera[1, 1] * p1 + camera[1, 2] * p2 + camera[1, 3]
    falloff = 0.5 / (scales * scales)
    opaque = 1.0 / (1.0 + jnp.exp(-opacity))
    stack = jnp.concatenate([mean_x, mean_y, falloff, opaque], axis=0)
    return reorder(stack.astype(bf16), False)


def screen_rows(stack):
    rows = [stack[k * BINS + b : k * BINS + b + 1] for b in range(BINS) for k in range(4)]
    return jnp.concatenate(rows, axis=0).astype(bf16)


def spread(stack, screen):
    rows = screen_rows(stack)
    for t in range(N_TILE):
        screen[t] = rows


def fetch(pairs, sems):
    copies = [pltpu.make_async_copy(source, to, sems.at[i]) for i, (source, to) in enumerate(pairs)]
    for copy in copies:
        copy.start()
    return copies


def prep_kernel(camera_hbm, owner_hbm, feat_hbm, pos_hbm, scales_hbm, opacity_hbm, colors, screen, geometry, *scratch):
    camera, owner, feat, pos, scales, opacity, sems = scratch
    copies = fetch(
        [
            (camera_hbm, camera),
            (owner_hbm, owner),
            (feat_hbm, feat),
            (pos_hbm, pos),
            (scales_hbm, scales),
            (opacity_hbm, opacity),
        ],
        sems,
    )
    for copy in copies:
        copy.wait()
    flat = feat[...].reshape(BINS * C, GB).astype(bf16)
    colors[...] = reorder(flat, False).astype(bf16).reshape(BINS, C, GB)
    stack = project_rows(pos[0], pos[1], pos[2], scales[...], opacity[...], camera.at[0])
    spread(stack, screen)
    for s in range(BINS):
        rows = [pos[k, s : s + 1] for k in range(3)]
        rows += [scales[s : s + 1], opacity[s : s + 1], jnp.zeros((3, GB), f32)]
        geometry[owner[s]] = jnp.concatenate(rows, axis=0)


def prep(camera, owner, feat, pos, scales, opacity):
    return pl.pallas_call(
        prep_kernel,
        out_shape=(
            jax.ShapeDtypeStruct((BINS, C, GB), bf16),
            jax.ShapeDtypeStruct((N_TILE, BINS * 4, GB), bf16),
            jax.ShapeDtypeStruct((N_VIEW, 8, GB), f32),
        ),
        in_specs=[ANY] * 6,
        out_specs=(VM, VM, VM),
        scratch_shapes=[
            pltpu.SMEM((1, 2, 4), f32),
            pltpu.SMEM((BINS,), jnp.int32),
            pltpu.VMEM((BINS, C, GB), f32),
            pltpu.VMEM((3, BINS, GB), f32),
            pltpu.VMEM((BINS, GB), f32),
            pltpu.VMEM((BINS, GB), f32),
            pltpu.SemaphoreType.DMA((6,)),
        ],
        compiler_params=params(60),
        name="prep",
    )(camera, owner, feat, pos, scales, opacity)


def screen_kernel(camera, geometry, screen):
    rows = [jnp.concatenate([geometry[b, k : k + 1] for b in range(BINS)], axis=0) for k in range(5)]
    spread(project_rows(*rows, camera), screen)


def screen_again(camera, geometry):
    return pl.pallas_call(
        screen_kernel,
        out_shape=jax.ShapeDtypeStruct((N_TILE, BINS * 4, GB), bf16),
        in_specs=[SM, VM],
        out_specs=VM,
        compiler_params=params(8),
        name="screen_again",
    )(camera, geometry)


def weights_kernel(lists_hbm, loads_hbm, shift_hbm, screen_hbm, out_hbm, token, *scratch):
    lists, loads, shift, screen, bins, out, work, sem, sems = scratch
    copies = fetch([(lists_hbm, lists), (loads_hbm, loads), (shift_hbm, shift), (screen_hbm, screen)], sems)
    token[...] = jnp.zeros((8, GB), jnp.int32)
    row = lax.broadcasted_iota(jnp.int32, (8, GB), 0)
    lane = lax.broadcasted_iota(jnp.int32, (8, GB), 1)
    pixel_x = (lane % SIDE).astype(f32) + 0.5
    pixel_y = (lane // SIDE).astype(f32) + 0.5
    for copy in copies:
        copy.wait()

    def widen(t, unused):
        rows = screen[t].astype(f32)
        for i in range(BINS // 2):
            two = rows[8 * i : 8 * i + 8]
            bins[t * BINS + 2 * i] = two
            bins[t * BINS + 2 * i + 1] = pltpu.roll(two, 4, 0)
        return unused

    lax.fori_loop(0, N_TILE, widen, 0, unroll=4)
    source = lax.broadcasted_iota(jnp.int32, (GROUP * 8, 4 * GB), 0)
    wanted = lax.broadcasted_iota(jnp.int32, (GROUP * 8, 4 * GB), 1) // GB

    def one(wide, place_x, place_y):
        running = [jnp.ones((8, GB), f32) for half in range(2)]
        parts = [[], []]
        for v in range(ROWS):
            some = wide[v * 8 : v * 8 + 8]
            mean_x, mean_y, fall, opaque = (some[:, k * GB : k * GB + GB] for k in range(4))
            fall = fall * -LOG2E
            delta_x = place_x - mean_x
            along_x = delta_x * delta_x * fall
            for half in range(2):
                delta_y = place_y[half] - mean_y
                part = opaque * jnp.exp2(along_x + delta_y * delta_y * fall) * running[half]
                parts[half].append(part)
                running[half] = running[half] - part
        before, after = [], []
        for total in running:
            for step in (1, 2, 4):
                total = total * jnp.where(row >= step, pltpu.roll(total, step, 0), 1.0)
            before.append(jnp.where(row >= 1, pltpu.roll(total, 1, 0), 1.0))
            after.append(jnp.broadcast_to(total[7:8], (8, GB)))
        return parts, before, after

    def plan(tile, state):
        count, spare = state
        live = loads[tile]
        for q in range(LBLK):
            work[count + q] = tile * LBLK + q
        return count + live, jnp.where(live < LBLK, tile * LBLK + LBLK - 1, spare)

    count, spare = lax.fori_loop(0, TILES, plan, (0, 0))
    for k in range(GROUP):
        work[count + k] = spare

    def leave(item):
        return pltpu.make_async_copy(out.at[item], out_hbm.at[item // LBLK, item % LBLK], sem)

    def group(step, carried):
        items = [work[step * GROUP + k] for k in range(GROUP)]
        done, values = [], []
        for item in items:
            tile, q = item // LBLK, item % LBLK
            alive = jnp.where(q < loads[tile], 1.0, 0.0)
            value = bins[lists[q, tile]]
            values.append(jnp.where(row == 3, value * alive, value))
        columns = jnp.concatenate(values, axis=0).T.astype(bf16)
        for k, item in enumerate(items):
            tile = item // LBLK
            pick = jnp.where(source == wanted + 8 * k, 1.0, 0.0).astype(bf16)
            wide = jnp.dot(columns, pick, preferred_element_type=f32)
            place_x = pixel_x + shift[0, tile]
            place_y = [pixel_y + shift[1, tile] + 8.0 * half for half in range(2)]
            done.append(one(wide, place_x, place_y))
        for item, (parts, before, after) in zip(items, done):
            fresh = item % LBLK == 0
            carried = [jnp.where(fresh, 1.0, value) for value in carried]
            for half in range(2):
                scale = carried[half] * before[half]
                rows = [part * scale for part in parts[half]]
                out[item, :, half * GB : half * GB + GB] = jnp.concatenate(rows, axis=0).astype(bf16)
            carried = [carried[half] * after[half] for half in range(2)]
        for k, item in enumerate(items):

            @pl.when(step * GROUP + k < count)
            def _():
                leave(item).start()

        return tuple(carried)

    lax.fori_loop(0, (count + GROUP - 1) // GROUP, group, (jnp.ones((8, GB), f32),) * 2)

    def arrived(i, unused):
        leave(0).wait()
        return unused

    lax.fori_loop(0, count, arrived, 0)


def weights(lists, loads, shift, screen, name):
    return pl.pallas_call(
        weights_kernel,
        out_shape=(jax.ShapeDtypeStruct((TILES, LBLK, GB, PIX), bf16), jax.ShapeDtypeStruct((8, GB), jnp.int32)),
        in_specs=[ANY] * 4,
        out_specs=(ANY, VM),
        scratch_shapes=[
            pltpu.SMEM((LBLK, TILES), jnp.int32),
            pltpu.SMEM((TILES,), jnp.int32),
            pltpu.SMEM((2, TILES), f32),
            pltpu.VMEM((N_TILE, BINS * 4, GB), bf16),
            pltpu.VMEM((N_TILE * BINS, 8, GB), f32),
            pltpu.VMEM((TILES * LBLK, GB, PIX), bf16),
            pltpu.SMEM((TILES * LBLK + LBLK,), jnp.int32),
            pltpu.SemaphoreType.DMA,
            pltpu.SemaphoreType.DMA((4,)),
        ],
        compiler_params=params(WEIGHTS_MIB),
        cost_estimate=pl.CostEstimate(
            flops=TILES * LBLK * GB * PIX * 14, bytes_accessed=10_000_000, transcendentals=TILES * LBLK * GB * PIX
        ),
        name=name,
    )(lists.T, loads, shift.T, screen)


def load_colors(blocks, colors, sems):
    return fetch([(block, colors.at[pl.ds(i * 32, 32)]) for i, block in enumerate(blocks)], sems)


def fetch_weights(loads, w_hbm, w, sems):
    def tile_start(tile, unused):
        for q in range(LBLK):

            @pl.when(q < loads[tile])
            def _():
                pltpu.make_async_copy(w_hbm.at[tile, q], w.at[tile, q], sems.at[tile]).start()

        return unused

    lax.fori_loop(0, TILES, tile_start, 0)


def over_tiles(loads, w_hbm, w, sems, body):
    def each_tile(tile, unused):
        live = loads[tile]
        for size in range(1, LBLK + 1):

            @pl.when(live == size)
            def _():
                pltpu.make_async_copy(
                    w_hbm.at[tile, pl.ds(0, size)], w.at[tile, pl.ds(0, size)], sems.at[tile]
                ).wait()
                body(tile, w[tile, :size].reshape(size * GB, PIX), size)

        return unused

    lax.fori_loop(0, TILES, each_tile, 0)


def picture(slots, tile, w, size, colors):
    row = jnp.concatenate([colors[slots[tile, q]] for q in range(size)], axis=1)
    return jnp.dot(row, w, preferred_element_type=f32)


def first_kernel(slots, loads, w_hbm, target_hbm, *rest):
    blocks, outs, (colors, w, target, total, sems, w_sems, t_sem) = rest[:8], rest[8:16], rest[16:]
    copies = load_colors(blocks, colors, sems) + fetch([(target_hbm, target)], t_sem)
    fetch_weights(loads, w_hbm, w, w_sems)

    def clear(i, unused):
        total[pl.ds(i * 8, 8)] = jnp.zeros((8, C, GB), f32)
        return unused

    lax.fori_loop(0, N_TILE, clear, 0)
    for copy in copies:
        copy.wait()

    def body(tile, w, size):
        residual = (picture(slots, tile, w, size, colors) - target[tile].astype(f32)).astype(bf16)
        pieces = lax.dot_general(residual, w, (((1,), (1,)), ((), ())), preferred_element_type=f32)
        for q in range(size):
            slot = slots[tile, q]
            total[slot] = total[slot] + pieces[:, q * GB : q * GB + GB]

    over_tiles(loads, w_hbm, w, w_sems, body)
    copies = fetch([(total.at[pl.ds(i * 32, 32)], out) for i, out in enumerate(outs)], sems)
    for copy in copies:
        copy.wait()


def first_render(slots, loads, w, target, blocks):
    return pl.pallas_call(
        first_kernel,
        out_shape=(jax.ShapeDtypeStruct((32, C, GB), f32),) * 8,
        in_specs=[SM, SM, ANY, ANY] + [ANY] * 8,
        out_specs=(ANY,) * 8,
        scratch_shapes=[
            pltpu.VMEM((N_TILE * BINS, C, GB), bf16),
            pltpu.VMEM((TILES, LBLK, GB, PIX), bf16),
            pltpu.VMEM((TILES, C, PIX), bf16),
            pltpu.VMEM((N_TILE * BINS, C, GB), f32),
            pltpu.SemaphoreType.DMA((8,)),
            pltpu.SemaphoreType.DMA((TILES,)),
            pltpu.SemaphoreType.DMA((1,)),
        ],
        compiler_params=params(RENDER_MIB),
        cost_estimate=pl.CostEstimate(flops=TILES * LBLK * C * GB * PIX * 4, bytes_accessed=25_000_000, transcendentals=0),
        name="first_render",
    )(slots, loads, w, target, *blocks)


def second_kernel(slots, loads, w_hbm, packed, *rest):
    blocks, image, news, (colors, w, sems, w_sems, n_sems) = rest[:8], rest[8], rest[9:12], rest[12:]
    copies = load_colors(blocks, colors, sems)
    fetch_weights(loads, w_hbm, w, w_sems)
    moves = fetch([(packed.at[:, pl.ds(i * C, C)], new) for i, new in enumerate(news)], n_sems)
    for copy in copies:
        copy.wait()

    def body(tile, w, size):
        image[tile] = picture(slots, tile, w, size, colors)

    over_tiles(loads, w_hbm, w, w_sems, body)
    for move in moves:
        move.wait()


def second_render(slots, loads, w, packed, blocks):
    wide = jax.ShapeDtypeStruct((BINS, C, GB), f32)
    return pl.pallas_call(
        second_kernel,
        out_shape=(jax.ShapeDtypeStruct((TILES, C, PIX), f32), wide, wide, wide),
        in_specs=[SM, SM, ANY, ANY] + [ANY] * 8,
        out_specs=(VM, ANY, ANY, ANY),
        scratch_shapes=[
            pltpu.VMEM((N_TILE * BINS, C, GB), bf16),
            pltpu.VMEM((TILES, LBLK, GB, PIX), bf16),
            pltpu.SemaphoreType.DMA((8,)),
            pltpu.SemaphoreType.DMA((TILES,)),
            pltpu.SemaphoreType.DMA((3,)),
        ],
        compiler_params=params(SECOND_MIB),
        cost_estimate=pl.CostEstimate(flops=TILES * LBLK * C * GB * PIX * 2, bytes_accessed=14_000_000, transcendentals=0),
        name="second_render",
    )(slots, loads, w, packed, *blocks)


def adam_kernel(owner, me, gradient, feat, m1, m2, *rest):
    outs, packed, colors = rest[:N_VIEW], rest[N_VIEW], rest[N_VIEW + 1]
    g = reorder_wide(gradient[...].reshape(BINS * C, GB), True).reshape(BINS, C, GB)
    first_new = beta_first * m1[...] + (1.0 - beta_first) * g
    second_new = beta_second * m2[...] + (1.0 - beta_second) * g * g
    stepped = feat[...] - learn_rate * (first_new / bias_first) / (jnp.sqrt(second_new / bias_second) + adam_epsilon)
    flat = stepped.reshape(BINS * C, GB).astype(bf16)
    sent = reorder(flat, False).astype(bf16).reshape(BINS, C, GB)
    for s in range(BINS):
        w = owner[s]
        colors[w ^ me[0]] = sent[s]
        packed[w, 0:C] = stepped[s]
        packed[w, C : 2 * C] = first_new[s]
        packed[w, 2 * C : 3 * C] = second_new[s]
    for r, out in enumerate(outs):
        out[...] = colors[r : r + 1]


def adam(owner, me, gradient, feat, m1, m2):
    return pl.pallas_call(
        adam_kernel,
        out_shape=(
            *(jax.ShapeDtypeStruct((1, C, GB), bf16),) * N_VIEW,
            jax.ShapeDtypeStruct((N_VIEW, 3 * C, GB), f32),
        ),
        in_specs=[SM, SM, VM, VM, VM, VM],
        out_specs=(VM,) * (N_VIEW + 1),
        scratch_shapes=[pltpu.VMEM((N_VIEW, C, GB), bf16)],
        compiler_params=params(16),
        name="adam",
    )(owner, me, gradient, feat, m1, m2)


def device(x, y, c):
    return ((x % 4) * 4 + y % 4) * 2 + c


def shift_by(value, level, k):
    pairs = []
    for x in range(4):
        for y in range(4):
            for c in range(2):
                dx, dy = (k, 0) if c == level else (0, k)
                pairs.append((device(x, y, c), device(x + dx, y + dy, c)))
    return lax.ppermute(value, "tile", pairs)


def swap_core(value):
    pairs = [(t, t ^ 1) for t in range(N_TILE)]
    return lax.ppermute(value, "tile", pairs)


ORDER = (2, 1, 3)


def tie(*values):
    return lax.optimization_barrier(values)


def gather_line(colors):
    near = {0: colors}
    for k in ORDER:
        near[k] = shift_by(colors, 0, k)
    return jnp.concatenate([near[k] for k in range(4)], axis=0)


def gather_plane(line, later=None):
    plane = {0: line}
    for k in ORDER:
        if later is not None and k == ORDER[-1]:
            line, later = tie(line, later)
        plane[k] = shift_by(line, 1, k)
    own = [plane[k] for k in range(4)]
    return own if later is None else (own, later)


def swapped(own):
    return list(own) + [swap_core(block) for block in own]


def scatter_far(parts, later):
    half16 = jnp.float16
    sent = {}
    for k in ORDER:
        sent[k] = (parts[k] + swap_core(parts[4 + k])).astype(half16)
    line = parts[0] + swap_core(parts[4])
    sent[3], later = tie(sent[3], later)
    for k in ORDER:
        line = line + shift_by(sent[k], 1, -k).astype(f32)
    return line, later


def scatter_near(line):
    half16 = jnp.float16
    total = line[0:BINS]
    for k in ORDER:
        total = total + shift_by(line[k * BINS : (k + 1) * BINS].astype(half16), 0, -k).astype(f32)
    return total


def color_slots(lists, within):
    me = lax.axis_index("tile")
    x, y, c = me // 8, (me // 2) % 4, me % 2
    owner = lists // BINS
    far_x = (x - owner // 8) % 4
    far_y = (y - (owner // 2) % 4) % 4
    core = owner % 2
    near = jnp.where(core == 0, far_x, far_y)
    far = jnp.where(core == 0, far_y, far_x)
    return (((core ^ c) * 4 + far) * 4 + near) * BINS + within


def exchange_views(colors, later):
    got = {0: colors[0]}
    for i, r in enumerate((4, 5, 3, 6, 2, 7, 1)):
        value = colors[r]
        if i == LATER:
            value, later = tie(value, later)
        got[r] = lax.ppermute(value, "view", [(v, v ^ r) for v in range(N_VIEW)])
    return jnp.concatenate([got[r] for r in range(N_VIEW)], axis=0), later


def place_of(view):
    return view ^ lax.axis_index("view")


def across_view(value):
    return lax.all_to_all(value, "view", split_axis=0, concat_axis=0, tiled=True)


def across_tile(value):
    return lax.all_to_all(value, "tile", split_axis=0, concat_axis=0, tiled=True)


def local(
    features,
    moment_first,
    moment_second,
    positions,
    scales,
    opacity,
    cameras_first,
    shift_first,
    lists_first,
    loads_first,
    target,
    owner_after,
    cameras_second,
    shift_second,
    lists_second,
    loads_second,
):
    positions = jnp.transpose(positions, (1, 0, 2))
    colors, screen, geometry = prep(cameras_first, owner_after, features, positions, scales, opacity)
    screen = across_tile(screen)
    own, screen = gather_plane(gather_line(colors), screen)
    w_first, token = weights(lists_first[0], loads_first[0], shift_first[0], screen, "weights_first")
    line, *own = own
    *own, token = tie(*own, token)
    slots = color_slots(lists_first[0], lists_first[0] % BINS) + token[0:1, 0:LBLK]
    parts = first_render(slots, loads_first[0], w_first, target[0], swapped([line] + own))
    line, geometry = scatter_far(parts, geometry)
    screen = screen_again(cameras_second[0], across_view(geometry))
    line, screen = tie(line, screen)
    screen = across_tile(screen)
    gradient = scatter_near(line)
    me = lax.axis_index("view").reshape(1)
    *colors, packed = adam(owner_after, me, gradient, features, moment_first, moment_second)
    colors, screen = exchange_views(colors, screen)
    colors, packed = tie(colors, packed)
    w_second, token = weights(lists_second[0], loads_second[0], shift_second[0], screen, "weights_second")
    packed = across_view(packed)
    line, *own = gather_plane(gather_line(colors))
    *own, token = tie(*own, token)
    blocks = swapped([line] + own)
    slots = color_slots(lists_second[0], place_of(lists_second[0] % BINS)) + token[0:1, 0:LBLK]
    image, new_features, new_first, new_second = second_render(
        slots, loads_second[0], w_second, packed, blocks
    )
    return (image[None], new_features, new_first, new_second)


def solution(mesh):
    return jax.shard_map(
        local,
        mesh=mesh,
        in_specs=(
            P(("view", "tile"), None, None),
            P(("view", "tile"), None, None),
            P(("view", "tile"), None, None),
            P(("view", "tile"), None, None),
            P(("view", "tile"), None),
            P(("view", "tile"), None),
            P("view", None, None),
            P("view", "tile", None),
            P("view", "tile", None),
            P("view", "tile"),
            P("view", "tile", None, None),
            P(("view", "tile")),
            P("view", None, None),
            P("view", "tile", None),
            P("view", "tile", None),
            P("view", "tile"),
        ),
        out_specs=(
            P("view", "tile", None, None),
            P(("view", "tile"), None, None),
            P(("view", "tile"), None, None),
            P(("view", "tile"), None, None),
        ),
        check_vma=False,
    )
```
